32 devices in a mesh: groups: 2 (over x), expert: 16 (over z, y, core).
Axes of the slice: x: 2, y: 2, z: 4, core: 2. Of those that a mesh axis runs over, the one named last changes fastest.
Arguments:
- down_proj: bfloat16 [32, 768, 4096], P(('groups', 'expert')), parts along dimension 0, may hold values from -0.21875 to 0.21875
- cov_factor: bfloat16 [32, 768, 768], P(('groups', 'expert')), parts along dimension 0, as said below
- sketch: bfloat16 [32, 768, 256], P(('groups', 'expert')), parts along dimension 0, may hold values from -6 to 6
- membership: int32 [32], P('groups'), parts along dimension 0, may hold values from 0 to 7, as said below
Outputs:
- coef: bfloat16 [32, 768, 256], P(('groups', 'expert')), parts along dimension 0
- basis: bfloat16 [16, 4096, 256], P('groups', 'expert'), parts along dimension 0
The draws below stay inside these ranges and needn't reach their ends.
There are 2 independent parts, one for each index of `groups`. The reference program is written for one: setup_inputs(seed, part) draws one part's arguments, and reference() takes and returns one part's arrays. A program takes and returns all parts, laid end to end along the dimension named above; each array names one. Nothing has to cross between parts.
Inputs may be any that keep to these rules, and one draw needn't show every extreme that they name: `membership`: every cluster has one or more experts; cluster sizes differ. `cov_factor`: lower triangular with a positive diagonal.
All inputs are finite; a program needn't handle non-finite values.
Results may differ from the reference program's by a relative error of at most 0.0078.
Values may be sent and summed in bfloat16 or wider, within the bound.
No kernel may reach another device: no remote copies, remote signals or barrier semaphores. Data moves between devices by JAX's collectives and lax.ppermute only.
A program may use at most 64 MiB of HBM per device.

```python
import math
import jax
import jax.numpy as jnp
from jax import lax

D = 4096
H = 768
R = 256
EXPERTS = 16
CLUSTERS = 8


def draw_cov_factor(key, part):
    key = jax.random.fold_in(key, 11)
    first_key, second_key = jax.random.split(key)
    diagonal = jnp.exp(jax.random.uniform(first_key, (EXPERTS, H), jnp.float32, jnp.log(0.5), jnp.log(2.0)))
    spread = jax.random.normal(second_key, (EXPERTS, H, H), jnp.float32) * (0.8 / jnp.sqrt(H * 1.0))
    row_index = jnp.arange(H)[:, None]
    col_index = jnp.arange(H)[None, :]
    lower = (row_index > col_index).astype(jnp.float32)
    ident = (row_index == col_index).astype(jnp.float32)
    factor = spread * lower[None] + diagonal[:, :, None] * ident[None]
    return factor.astype(jnp.bfloat16)


def draw_membership(key, part):
    key = jax.random.fold_in(key, 23)
    first_key, second_key = jax.random.split(key)
    order = jax.random.permutation(first_key, CLUSTERS)
    index = jnp.arange(CLUSTERS)
    extra = jnp.where(index < 3, order[0], order[1 + index % (CLUSTERS - 1)])
    slots = jnp.concatenate([index, extra]).astype(jnp.int32)
    shuffle = jax.random.permutation(second_key, EXPERTS)
    return slots[shuffle].astype(jnp.int32)


def shard_levels(own_key, dims, pieces, smallest, top_value):
    level = 1.0
    for position, blocks in pieces:
        steps = jax.random.uniform(jax.random.fold_in(jax.random.fold_in(own_key, 6), position), (blocks,), jnp.float32, smallest / len(pieces), top_value / len(pieces))
        level = level * jnp.repeat(jnp.exp(steps), dims[position] // blocks).reshape((-1,) + (1,) * (len(dims) - 1 - position))
    return level


def normal_values(rng, shape, scale, bound, shards=(), held_as=jnp.bfloat16):
    result = scale * jax.random.normal(rng, shape, jnp.float32)
    if shards:
        result = result * shard_levels(rng, shape, shards, -0.22, 0.18)
    return jnp.clip(result, -bound, bound).astype(held_as)


def setup_inputs(seed: int = 0, part: int = 0) -> dict:
    arg_keys = jax.random.split(jax.random.key(seed), 5)
    part_splits = jax.random.split(jax.random.fold_in(arg_keys[4], part), 5)
    return {
        "down_proj": normal_values(part_splits[0], (EXPERTS, H, D), H ** -0.5, 0.21875, ((0, 16),)),
        "cov_factor": draw_cov_factor(jax.random.fold_in(jax.random.fold_in(arg_keys[4], part), 71), part),
        "sketch": normal_values(part_splits[2], (EXPERTS, H, R), 1.0, 6.0, ((0, 16),)),
        "membership": draw_membership(jax.random.fold_in(jax.random.fold_in(arg_keys[4], part), 71), part),
    }


def local_gram(rows):
    return jnp.dot(rows.T.astype(jnp.float32), rows.astype(jnp.float32), preferred_element_type=jnp.float32)

def orthonormal_rows(rows, total_gram):
    factor = jnp.linalg.cholesky(total_gram)
    return jax.scipy.linalg.solve_triangular(factor, rows.T, lower=True).T

def reference(down_proj, cov_factor, sketch, membership):
    experts = down_proj.shape[0]
    width = down_proj.shape[2]
    rank_cols = sketch.shape[2]
    clusters = experts // 2

    def partial_of(items):
        weights, factor, draws = items
        weighted = jnp.dot(factor.astype(jnp.float32), draws.astype(jnp.float32), preferred_element_type=jnp.float32).astype(jnp.bfloat16)
        return jnp.dot(weights.T.astype(jnp.float32), weighted.astype(jnp.float32), preferred_element_type=jnp.float32).astype(jnp.bfloat16)
    partials = lax.map(partial_of, (down_proj, cov_factor, sketch))
    table = (membership[None, :] == jnp.arange(clusters, dtype=jnp.int32)[:, None]).astype(jnp.bfloat16)
    stacked = jnp.dot(table.astype(jnp.float32), partials.reshape(experts, width * rank_cols).astype(jnp.float32), preferred_element_type=jnp.float32)
    stacked = stacked.astype(jnp.bfloat16).reshape(clusters, width, rank_cols)

    def basis_of(rows):
        gram = local_gram(rows)
        single = orthonormal_rows(rows.astype(jnp.float32), gram)
        return (math.sqrt(width) * single).astype(jnp.bfloat16)
    basis = lax.map(basis_of, stacked)

    def coef_of(items):
        weights, index = items
        return jnp.dot(weights.astype(jnp.float32), basis[index].astype(jnp.float32), preferred_element_type=jnp.float32).astype(jnp.bfloat16)
    coef = lax.map(coef_of, (down_proj, membership))
    return (coef, basis)
```

```python
import functools
import math

import jax
import jax.numpy as jnp
from jax import lax
from jax.experimental import pallas as pl
from jax.experimental.pallas import tpu as pltpu
from jax.sharding import PartitionSpec as P

F32 = jnp.float32
BF16 = jnp.bfloat16
VMEM_LIMIT = 48 * 1024 * 1024
PANEL = 8
BLOCK = 64


def dot(a, b, dims):
    return lax.dot_general(a, b, (dims, ((), ())), preferred_element_type=F32)


def params():
    return pltpu.CompilerParams(vmem_limit_bytes=VMEM_LIMIT)


def partial_kernel(cov_ref, sketch_ref, weights_ref, out_ref, weighted):
    @pl.when(pl.program_id(0) == 0)
    def _():
        weighted[...] = dot(sketch_ref[...], cov_ref[...], ((0,), (1,))).astype(BF16)

    product = dot(weighted[...], weights_ref[...], ((1,), (0,))).astype(BF16)
    rows = out_ref.shape[2]
    for piece in range(out_ref.shape[0]):
        out_ref[piece] = product[:, piece * rows : (piece + 1) * rows]


def partial_blocks(cov, sketch, weights, devices):
    hidden, width = weights.shape
    rank = sketch.shape[1]
    rows = width // devices
    columns = min(width, 512)
    return pl.pallas_call(
        partial_kernel,
        grid=(width // columns,),
        in_specs=[
            pl.BlockSpec((hidden, hidden), lambda i: (0, 0)),
            pl.BlockSpec((hidden, rank), lambda i: (0, 0)),
            pl.BlockSpec((hidden, columns), lambda i: (0, i)),
        ],
        out_specs=pl.BlockSpec((columns // rows, rank, rows), lambda i: (i, 0, 0)),
        out_shape=jax.ShapeDtypeStruct((devices, rank, rows), BF16),
        scratch_shapes=[pltpu.VMEM((rank, hidden), BF16)],
        compiler_params=params(),
        cost_estimate=pl.CostEstimate(
            flops=2 * hidden * rank * (hidden + width),
            bytes_accessed=2 * (hidden * (width + hidden + rank) + rank * width),
            transcendentals=0,
        ),
    )(cov, sketch, weights)


def cluster_kernel(member_ref, base_ref, recv_ref, rows_ref, chosen_ref, keep_ref, send_ref, total):
    devices = recv_ref.shape[0]
    clusters = rows_ref.shape[0]
    half = rows_ref.shape[1] // 2
    total[...] = jnp.zeros_like(total)

    @pl.loop(0, devices)
    def _(e):
        c = member_ref[e]
        total[c] = total[c] + recv_ref[e].astype(F32)

    @pl.loop(0, clusters)
    def _(c):
        rows_ref[c] = total[c].astype(BF16)

    @pl.loop(0, devices)
    def _(e):
        chosen_ref[e] = rows_ref[member_ref[e]]

    def gram(slot):
        block = rows_ref[base_ref[0] ^ slot]
        full = dot(block, block, ((1,), (1,)))
        return full[:half, :half], full[half:, :half], full[half:, half:]

    kept = keep_ref.shape[0]

    @pl.loop(0, kept)
    def _(k):
        keep_ref[k, 0], keep_ref[k, 1], keep_ref[k, 2] = gram(k)
        send_ref[k, 0], send_ref[k, 1], send_ref[k, 2] = gram(k + kept)


def cluster_sums(members, base, received):
    devices, rank, rows = received.shape
    clusters = devices // 2
    half = rank // 2
    smem = pl.BlockSpec(memory_space=pltpu.SMEM)
    vmem = pl.BlockSpec(memory_space=pltpu.VMEM)
    gram = jax.ShapeDtypeStruct((clusters // 2, 3, half, half), F32)
    return pl.pallas_call(
        cluster_kernel,
        in_specs=[smem, smem, vmem],
        out_specs=[vmem] * 4,
        out_shape=[
            jax.ShapeDtypeStruct((clusters, rank, rows), BF16),
            jax.ShapeDtypeStruct((devices, rank, rows), BF16),
            gram,
            gram,
        ],
        scratch_shapes=[pltpu.VMEM((clusters, rank, rows), F32)],
        compiler_params=params(),
    )(members, base, received)


def stacked(x, axis, order):
    high = x.astype(BF16)
    rest = x - high.astype(F32)
    middle = rest.astype(BF16)
    low = (rest - middle.astype(F32)).astype(BF16)
    return jnp.concatenate([(high, middle, low)[i] for i in order], axis=axis)


def stack_left(x, axis):
    return stacked(x, axis, (0, 0, 1, 0, 2, 1))


def stack_right(x, axis):
    return stacked(x, axis, (0, 1, 0, 2, 0, 1))


def block_inverse(square):
    size = square.shape[0]
    lanes = 128
    groups = size // 8
    row = lax.broadcasted_iota(jnp.int32, (size, size), 0)
    col = lax.broadcasted_iota(jnp.int32, (size, size), 1)
    parts = [square, jnp.where(row == col, 1.0, 0.0)]
    if lanes > 2 * size:
        parts.append(jnp.zeros((size, lanes - 2 * size), F32))
    table = jnp.concatenate(parts, axis=1)
    tiles = [table[8 * g : 8 * g + 8, :] for g in range(groups)]
    sub = lax.broadcasted_iota(jnp.int32, (8, lanes), 0)
    pivots = [jnp.ones((8, lanes), F32) for _ in range(groups)]

    def spread(x):
        return jnp.broadcast_to(x, (8, lanes))

    for k in range(0, size, PANEL):
        first = k // 8
        columns = [
            [spread(tiles[g][:, k + i : k + i + 1]) for g in range(first, groups)]
            for i in range(PANEL)
        ]
        s = {}
        for m in range(PANEL):
            for i in range(m, PANEL):
                q = k + i
                s[m, i] = spread(columns[m][q // 8 - first][q % 8 : q % 8 + 1, :])
        rows = [spread(tiles[(k + i) // 8][(k + i) % 8 : (k + i) % 8 + 1, :]) for i in range(PANEL)]
        inverse = []
        for m in range(PANEL):
            inverse.append(1.0 / s[m, m])
            for i in range(m + 1, PANEL):
                factor = s[m, i] * inverse[m]
                for t in range(i, PANEL):
                    s[i, t] = s[i, t] - factor * s[m, t]
                rows[i] = rows[i] - factor * rows[m]
        factors = []
        for m in range(PANEL):
            column = []
            for g in range(groups - first):
                x = columns[m][g]
                for t in range(m):
                    x = x - factors[t][g] * s[t, m]
                column.append(x * inverse[m])
            factors.append(column)
        for g in range(first, groups):
            tile = tiles[g]
            for m in range(PANEL):
                x = factors[m][g - first]
                if 8 * g <= k + m:
                    x = jnp.where(sub + 8 * g > k + m, x, 0.0)
                tile = tile - x * rows[m]
            tiles[g] = tile
        for m in range(PANEL):
            q = k + m
            pivots[q // 8] = jnp.where(sub == q % 8, s[m, m], pivots[q // 8])
    out = [tiles[g] * lax.rsqrt(pivots[g]) for g in range(groups)]
    return jnp.concatenate(out, axis=0)[:, size : 2 * size]


def inverse_kernel(scale, gram_ref, out_ref, work):
    half = gram_ref.shape[1]
    n = 2 * half
    row = lax.broadcasted_iota(jnp.int32, (n, n), 0)
    col = lax.broadcasted_iota(jnp.int32, (n, n), 1)
    work[:half, :half] = gram_ref[0]
    work[half:, :half] = gram_ref[1]
    work[:half, half:n] = gram_ref[1].T
    work[half:, half:n] = gram_ref[2]
    work[:, n:] = jnp.where(row == col, 1.0, 0.0)
    for top in range(0, n, BLOCK):
        left = top // 128 * 128
        bottom = top + BLOCK
        square = work[top:bottom, left : left + 128][:, top - left : bottom - left]
        scaled = dot(
            stack_left(block_inverse(square), 1), stack_right(work[top:bottom, :], 0), ((1,), (0,))
        )
        work[top:bottom, n:] = scaled[:, n:]
        if bottom < n:
            start = bottom // 128 * 128
            change = dot(
                stack_left(scaled[:, start:n], 0), stack_right(scaled, 0), ((0,), (0,))
            )
            work[bottom:, :] = work[bottom:, :] - change[bottom - start :, :]
    out_ref[0] = (scale * work[:half, n : n + half]).astype(out_ref.dtype)
    out_ref[1] = (scale * work[half:, n : n + half]).astype(out_ref.dtype)
    out_ref[2] = (scale * work[half:, n + half :]).astype(out_ref.dtype)


def inverse_factor(gram, scale):
    half = gram.shape[1]
    return pl.pallas_call(
        functools.partial(inverse_kernel, scale),
        out_shape=jax.ShapeDtypeStruct(gram.shape, BF16),
        scratch_shapes=[pltpu.VMEM((2 * half, 4 * half), F32)],
        compiler_params=params(),
    )(gram)


def basis_kernel(base_ref, rows_ref, inverse_ref, out_ref):
    half = inverse_ref.shape[2]

    @pl.loop(0, rows_ref.shape[0])
    def _(c):
        slot = base_ref[0] ^ c
        block = rows_ref[c]
        top = dot(inverse_ref[slot, 0], block[:half], ((1,), (0,)))
        bottom = dot(inverse_ref[slot, 1], block[:half], ((1,), (0,))) + dot(
            inverse_ref[slot, 2], block[half:], ((1,), (0,))
        )
        out_ref[c, :, :half] = top.T.astype(BF16)
        out_ref[c, :, half:] = bottom.T.astype(BF16)


def basis_rows(base, rows_t, inverses):
    clusters, rank, rows = rows_t.shape
    vmem = pl.BlockSpec(memory_space=pltpu.VMEM)
    return pl.pallas_call(
        basis_kernel,
        in_specs=[pl.BlockSpec(memory_space=pltpu.SMEM), vmem, vmem],
        out_specs=vmem,
        out_shape=jax.ShapeDtypeStruct((clusters, rows, rank), BF16),
        compiler_params=params(),
    )(base, rows_t, inverses)


def coef_kernel(slot_ref, weights_ref, gathered_ref, inverse_ref, out_ref, total):
    step = pl.program_id(0)
    rows = gathered_ref.shape[2]

    @pl.when(step == 0)
    def _():
        total[...] = jnp.zeros_like(total)

    block = weights_ref[...]
    for piece in range(gathered_ref.shape[0]):
        total[...] += dot(
            block[:, piece * rows : (piece + 1) * rows], gathered_ref[piece], ((1,), (1,))
        )

    @pl.when(step == pl.num_programs(0) - 1)
    def _():
        half = inverse_ref.shape[2]
        high = total[...].astype(BF16)
        low = (total[...] - high.astype(F32)).astype(BF16)
        slot = slot_ref[0]
        first, below, second = (inverse_ref[slot, i] for i in range(3))

        def times(cols, factor):
            return dot(high[:, cols], factor, ((1,), (1,))) + dot(low[:, cols], factor, ((1,), (1,)))

        left, right = slice(0, half), slice(half, 2 * half)
        out_ref[:, left] = times(left, first).astype(BF16)
        out_ref[:, right] = (times(left, below) + times(right, second)).astype(BF16)


def coefficients(slot, weights, gathered, inverses):
    hidden, width = weights.shape
    devices, rank, rows = gathered.shape
    columns = min(width, 512)
    return pl.pallas_call(
        coef_kernel,
        grid=(width // columns,),
        in_specs=[
            pl.BlockSpec(memory_space=pltpu.SMEM),
            pl.BlockSpec((hidden, columns), lambda i: (0, i)),
            pl.BlockSpec((columns // rows, rank, rows), lambda i: (i, 0, 0)),
            pl.BlockSpec(inverses.shape, lambda i: (0, 0, 0, 0)),
        ],
        out_specs=pl.BlockSpec((hidden, rank), lambda i: (0, 0)),
        out_shape=jax.ShapeDtypeStruct((hidden, rank), BF16),
        scratch_shapes=[pltpu.VMEM((hidden, rank), F32)],
        compiler_params=params(),
    )(slot, weights, gathered, inverses)


def swap(block, bit):
    count = lax.axis_size("expert")
    return lax.ppermute(block, "expert", [(i, i ^ (1 << bit)) for i in range(count)])


def exchange(blocks):
    return lax.all_to_all(blocks, "expert", split_axis=0, concat_axis=0, tiled=True)


def local(down_proj, cov_factor, sketch, membership):
    devices = lax.axis_size("expert")
    weights = down_proj[0]
    width = weights.shape[1]
    bits = devices.bit_length() - 1
    me = lax.axis_index("expert")
    base = sum(((me >> s) & 1) << (bits - 2 - s) for s in range(bits - 1)).astype(jnp.int32)
    slot = (membership[me] ^ base).reshape(1)
    base = base.reshape(1)

    received = exchange(partial_blocks(cov_factor[0], sketch[0], weights, devices))
    rows_t, chosen, keep, send = cluster_sums(membership, base, received)
    gathered = exchange(chosen)

    total = keep + swap(send, 0)
    for bit in range(1, bits - 1):
        kept = total.shape[0] // 2
        total = total[:kept] + swap(total[kept:], bit)
    total = total + swap(total, bits - 1)
    inverses = inverse_factor(total[0], math.sqrt(width))[None]
    for bit in reversed(range(bits - 1)):
        inverses = jnp.concatenate([inverses, swap(inverses, bit)], axis=0)

    basis = basis_rows(base, rows_t, inverses)
    coef = coefficients(slot, weights, gathered, inverses)
    return (coef[None], basis)


def solution(mesh):
    placed = (
        P(("groups", "expert"), None, None),
        P(("groups", "expert"), None, None),
        P(("groups", "expert"), None, None),
        P("groups"),
    )
    return jax.shard_map(
        local,
        mesh=mesh,
        in_specs=placed,
        out_specs=(P(("groups", "expert"), None, None), P("groups", "expert", None)),
        check_vma=False,
    )
```

```python
import functools
import math

import jax
import jax.numpy as jnp
from jax import lax
from jax.experimental import pallas as pl
from jax.experimental.pallas import tpu as pltpu
from jax.sharding import PartitionSpec as P

F32 = jnp.float32
BF16 = jnp.bfloat16
MIB = 1024 * 1024
PANEL = 8
BLOCK = 64
AHEAD = 6
PLAN = {"sum": (1, 1), "last": (0, 2), "invert": (2, 2), "share": (1, 1)}
VMEM = pl.BlockSpec(memory_space=pltpu.VMEM)
SMEM = pl.BlockSpec(memory_space=pltpu.SMEM)
HBM = pl.BlockSpec(memory_space=pltpu.MemorySpace.HBM)


def dot(a, b, dims):
    return lax.dot_general(a, b, (dims, ((), ())), preferred_element_type=F32)


def params(mib=24):
    return pltpu.CompilerParams(vmem_limit_bytes=mib * MIB)


def base_cluster(me, devices):
    last = devices.bit_length() - 2
    return sum(((me >> s) & 1) << (last - 1 - s) for s in range(last))


def weight_copies(me, weights_hbm, weights, sems, rows, half, far):
    quarter = half // 2
    columns = quarter * rows
    own = me // half
    first = (1 - own if far else own) * 2
    copies = []
    for part in range(2):
        start = (first + (me % half // quarter ^ part)) * columns
        copies.append(
            pltpu.make_async_copy(
                weights_hbm.at[:, pl.ds(pl.multiple_of(start, columns), columns)],
                weights.at[part],
                sems.at[part],
            )
        )
    return copies


def slot_blocks(me, weighted, weights, copy, part, product, outs):
    count = product.shape[0]
    rows = product.shape[2]
    copy.wait()
    wide = dot(weighted, weights[part], ((1,), (0,))).astype(BF16)
    for b in range(count):
        product[b] = wide[:, b * rows : (b + 1) * rows]
    for t in range(count):
        outs[part * count + t][...] = product[me % count ^ t]


def far_partial_kernel(half, ids_ref, cov_hbm, sketch_hbm, weights_hbm, *refs):
    outs, weighted_ref = refs[:half], refs[half]
    cov, sketch, weights, product, in_sems, sems = refs[half + 1 :]
    me = ids_ref[0]
    cov_copy = pltpu.make_async_copy(cov_hbm, cov, in_sems.at[0])
    sketch_copy = pltpu.make_async_copy(sketch_hbm, sketch, in_sems.at[1])
    copies = weight_copies(me, weights_hbm, weights, sems, product.shape[2], half, True)
    cov_copy.start()
    sketch_copy.start()
    copies[0].start()
    cov_copy.wait()
    sketch_copy.wait()
    copies[1].start()
    weighted = dot(sketch[...], cov[...], ((0,), (1,))).astype(BF16)
    weighted_ref[...] = weighted
    for part in range(2):
        slot_blocks(me, weighted, weights, copies[part], part, product, outs)


def near_partial_kernel(half, ids_ref, weighted_ref, weights_hbm, *refs):
    outs = refs[:half]
    weights, product, sems = refs[half:]
    me = ids_ref[0]
    copies = weight_copies(me, weights_hbm, weights, sems, product.shape[2], half, False)
    for copy in copies:
        copy.start()
    for part in range(2):
        slot_blocks(me, weighted_ref[...], weights, copies[part], part, product, outs)


def partial_blocks(ids, cov, sketch, weights, devices):
    hidden, width = weights.shape
    rank = sketch.shape[1]
    rows = width // devices
    half = devices // 2
    block = jax.ShapeDtypeStruct((rank, rows), BF16)
    scratch = [
        pltpu.VMEM((2, hidden, width // 4), BF16),
        pltpu.VMEM((half // 2, rank, rows), BF16),
    ]
    sems = pltpu.SemaphoreType.DMA((2,))
    *far, weighted = pl.pallas_call(
        functools.partial(far_partial_kernel, half),
        in_specs=[SMEM, HBM, HBM, HBM],
        out_specs=[VMEM] * (half + 1),
        out_shape=[block] * half + [jax.ShapeDtypeStruct((rank, hidden), BF16)],
        scratch_shapes=[pltpu.VMEM(cov.shape, BF16), pltpu.VMEM(sketch.shape, BF16)]
        + scratch
        + [sems, sems],
        compiler_params=params(62),
    )(ids, cov, sketch, weights)
    near = pl.pallas_call(
        functools.partial(near_partial_kernel, half),
        in_specs=[SMEM, VMEM, HBM],
        out_specs=[VMEM] * half,
        out_shape=[block] * half,
        scratch_shapes=scratch + [sems],
        compiler_params=params(),
    )(ids, weighted, weights)
    return [*near, *far]


def cluster_kernel(devices, ids_ref, member_ref, *refs):
    received, refs = refs[:devices], refs[devices:]
    rows_ref, keep_ref, send_ref = refs[:3]
    blocks, total = refs[3 : 3 + devices], refs[-1]
    me = ids_ref[0]
    base = base_cluster(me, devices)
    half = rows_ref.shape[1] // 2
    total[...] = jnp.zeros_like(total)
    for s in range(devices):
        c = member_ref[me ^ s]
        total[c] = total[c] + received[s][...].astype(F32)
    rows_ref[...] = total[...].astype(BF16)
    for s in range(devices):
        blocks[s][...] = rows_ref[member_ref[me ^ s]]
    kept = keep_ref.shape[0]

    @pl.loop(0, kept)
    def _(k):
        for out_ref, slot in ((send_ref, k + kept), (keep_ref, k)):
            block = rows_ref[base ^ slot]
            full = dot(block, block, ((1,), (1,)))
            out_ref[k, 0] = full[:half, :half]
            out_ref[k, 1] = full[half:, :half]
            out_ref[k, 2] = full[half:, half:]


def cluster_sums(ids, members, received):
    devices = len(received)
    clusters = devices // 2
    rank, rows = received[0].shape
    gram = jax.ShapeDtypeStruct((clusters // 2, 3, rank // 2, rank // 2), F32)
    block = jax.ShapeDtypeStruct((rank, rows), BF16)
    rows_t, keep, send, *blocks = pl.pallas_call(
        functools.partial(cluster_kernel, devices),
        in_specs=[SMEM, SMEM] + [VMEM] * devices,
        out_specs=[VMEM] * (devices + 3),
        out_shape=[jax.ShapeDtypeStruct((clusters, rank, rows), BF16), gram, gram]
        + [block] * devices,
        scratch_shapes=[pltpu.VMEM((clusters, rank, rows), F32)],
        compiler_params=params(),
    )(ids, members, *received)
    return rows_t, keep, send, blocks


def stacked(x, axis, order):
    high = x.astype(BF16)
    rest = x - high.astype(F32)
    middle = rest.astype(BF16)
    low = (rest - middle.astype(F32)).astype(BF16)
    return jnp.concatenate([(high, middle, low)[i] for i in order], axis=axis)


def stack_left(x, axis):
    return stacked(x, axis, (0, 0, 1, 0, 2, 1))


def stack_right(x, axis):
    return stacked(x, axis, (0, 1, 0, 2, 0, 1))


def block_inverse(square):
    size = square.shape[0]
    lanes = 128
    groups = size // 8
    row = lax.broadcasted_iota(jnp.int32, (size, size), 0)
    col = lax.broadcasted_iota(jnp.int32, (size, size), 1)
    parts = [square, jnp.where(row == col, 1.0, 0.0)]
    if lanes > 2 * size:
        parts.append(jnp.zeros((size, lanes - 2 * size), F32))
    table = jnp.concatenate(parts, axis=1)
    tiles = [table[8 * g : 8 * g + 8, :] for g in range(groups)]
    sub = lax.broadcasted_iota(jnp.int32, (8, lanes), 0)
    pivots = [jnp.ones((8, lanes), F32) for _ in range(groups)]

    def spread(x):
        return jnp.broadcast_to(x, (8, lanes))

    for k in range(0, size, PANEL):
        first = k // 8
        columns = [
            [spread(tiles[g][:, k + i : k + i + 1]) for g in range(first, groups)]
            for i in range(PANEL)
        ]
        s = {}
        for m in range(PANEL):
            for i in range(m, PANEL):
                q = k + i
                s[m, i] = spread(columns[m][q // 8 - first][q % 8 : q % 8 + 1, :])
        rows = [spread(tiles[(k + i) // 8][(k + i) % 8 : (k + i) % 8 + 1, :]) for i in range(PANEL)]
        inverse = []
        for m in range(PANEL):
            inverse.append(1.0 / s[m, m])
            for i in range(m + 1, PANEL):
                factor = s[m, i] * inverse[m]
                for t in range(i, PANEL):
                    s[i, t] = s[i, t] - factor * s[m, t]
                rows[i] = rows[i] - factor * rows[m]
        factors = []
        for m in range(PANEL):
            column = []
            for g in range(groups - first):
                x = columns[m][g]
                for t in range(m):
                    x = x - factors[t][g] * s[t, m]
                column.append(x * inverse[m])
            factors.append(column)
        for g in range(first, groups):
            tile = tiles[g]
            for m in range(PANEL):
                x = factors[m][g - first]
                if 8 * g <= k + m:
                    x = jnp.where(sub + 8 * g > k + m, x, 0.0)
                tile = tile - x * rows[m]
            tiles[g] = tile
        for m in range(PANEL):
            q = k + m
            pivots[q // 8] = jnp.where(sub == q % 8, s[m, m], pivots[q // 8])
    out = [tiles[g] * lax.rsqrt(pivots[g]) for g in range(groups)]
    return jnp.concatenate(out, axis=0)[:, size : 2 * size]


def invert(work):
    n = work.shape[0]
    for top in range(0, n, BLOCK):
        left = top // 128 * 128
        bottom = top + BLOCK
        square = work[top:bottom, left : left + 128][:, top - left : bottom - left]
        scaled = dot(
            stack_left(block_inverse(square), 1), stack_right(work[top:bottom, :], 0), ((1,), (0,))
        )
        work[top:bottom, n:] = scaled[:, n:]
        if bottom < n:
            start = bottom // 128 * 128
            change = dot(stack_left(scaled[:, start:n], 0), stack_right(scaled, 0), ((0,), (0,)))
            work[bottom:, :] = work[bottom:, :] - change[bottom - start :, :]


def identity(n):
    row = lax.broadcasted_iota(jnp.int32, (n, n), 0)
    col = lax.broadcasted_iota(jnp.int32, (n, n), 1)
    return jnp.where(row == col, 1.0, 0.0)


def inverse_kernel(scale, gram_ref, rows_t_ref, out_ref, rows_ref, work):
    for c in range(rows_ref.shape[0]):
        rows_ref[c] = rows_t_ref[c].T
    half = gram_ref.shape[1]
    n = 2 * half
    work[:half, :half] = gram_ref[0]
    work[half:, :half] = gram_ref[1]
    work[:half, half:n] = gram_ref[1].T
    work[half:, half:n] = gram_ref[2]
    work[:, n:] = identity(n)
    invert(work)
    out_ref[0] = (scale * work[:half, n : n + half]).astype(BF16)
    out_ref[1] = (scale * work[half:, n : n + half]).astype(BF16)
    out_ref[2] = (scale * work[half:, n + half :]).astype(BF16)


def inverse_factor(gram, rows_t, scale):
    half = gram.shape[1]
    clusters, rank, rows = rows_t.shape
    return pl.pallas_call(
        functools.partial(inverse_kernel, scale),
        in_specs=[VMEM] * 2,
        out_specs=[VMEM] * 2,
        out_shape=[
            jax.ShapeDtypeStruct(gram.shape, BF16),
            jax.ShapeDtypeStruct((clusters, rows, rank), BF16),
        ],
        scratch_shapes=[pltpu.VMEM((2 * half, 4 * half), F32)],
        compiler_params=params(),
    )(gram, rows_t)


def basis_kernel(ids_ref, rows_ref, near_ref, far_ref, out_hbm, out, sems):
    half = out.shape[2] // 2
    count = near_ref.shape[0]
    base = base_cluster(ids_ref[0], 4 * count)

    def copy(k):
        return pltpu.make_async_copy(out.at[k], out_hbm.at[base ^ k], sems.at[k])

    for k in range(2 * count):
        refs, i = (near_ref, k) if k < count else (far_ref, k - count)
        block = rows_ref[base ^ k]
        out[k, :, :half] = dot(block[:, :half], refs[i, 0], ((1,), (1,))).astype(BF16)
        out[k, :, half:] = (
            dot(block[:, :half], refs[i, 1], ((1,), (1,)))
            + dot(block[:, half:], refs[i, 2], ((1,), (1,)))
        ).astype(BF16)
        copy(k).start()
    for k in range(2 * count):
        copy(k).wait()


def basis_rows(ids, rows, near, far):
    return pl.pallas_call(
        basis_kernel,
        in_specs=[SMEM] + [VMEM] * 3,
        out_specs=HBM,
        out_shape=jax.ShapeDtypeStruct(rows.shape, BF16),
        scratch_shapes=[pltpu.VMEM(rows.shape, BF16), pltpu.SemaphoreType.DMA((rows.shape[0],))],
        compiler_params=params(),
    )(ids, rows, near, far)


def column_block(ref, index, rows):
    if rows % 128 == 0:
        return ref[:, pl.ds(pl.multiple_of(index * rows, rows), rows)]
    share = 128 // rows
    wide = ref[:, pl.ds(pl.multiple_of(index // share * 128, 128), 128)]
    block = wide[:, :rows]
    for i in range(1, share):
        block = jnp.where(index % share == i, wide[:, i * rows : (i + 1) * rows], block)
    return block


def first_product_kernel(ids_ref, weights_hbm, *refs):
    *blocks, out_ref, weights, sem = refs
    me = ids_ref[0]
    rows = blocks[0].shape[1]
    copy = pltpu.make_async_copy(weights_hbm, weights, sem)
    copy.start()
    copy.wait()
    total = None
    for s, block in enumerate(blocks):
        term = dot(column_block(weights, me ^ s, rows), block[...], ((1,), (1,)))
        total = term if total is None else total + term
    out_ref[...] = total


def coef_kernel(ids_ref, member_ref, weights_hbm, first_ref, near_ref, far_ref, *refs):
    *blocks, out_hbm, weights, out, sem, out_sem = refs
    me = ids_ref[0]
    slot = member_ref[me] ^ base_cluster(me, member_ref.shape[0])
    rows = blocks[0].shape[1]
    count = len(blocks)
    columns = count * rows
    start = (me // count ^ 3) * columns
    copy = pltpu.make_async_copy(
        weights_hbm.at[:, pl.ds(pl.multiple_of(start, columns), columns)], weights, sem
    )
    copy.start()
    copy.wait()
    total = first_ref[...]
    for t, block in enumerate(blocks):
        total = total + dot(
            column_block(weights, me % count ^ t, rows), block[...], ((1,), (1,))
        )
    high = total.astype(BF16)
    low = (total - high.astype(F32)).astype(BF16)
    near = slot < near_ref.shape[0]
    inside = lax.rem(slot, near_ref.shape[0])
    half = out.shape[1] // 2

    def times(i, part):
        factor = jnp.where(near, near_ref[inside, i], far_ref[inside, i])
        return dot(high[:, part], factor, ((1,), (1,))) + dot(low[:, part], factor, ((1,), (1,)))

    left, right = slice(0, half), slice(half, 2 * half)
    out[:, left] = times(0, left).astype(BF16)
    out[:, right] = (times(1, left) + times(2, right)).astype(BF16)
    out_copy = pltpu.make_async_copy(out, out_hbm, out_sem)
    out_copy.start()
    out_copy.wait()


def first_product(ids, weights, blocks):
    rank = blocks[0].shape[0]
    return pl.pallas_call(
        first_product_kernel,
        in_specs=[SMEM, HBM] + [VMEM] * len(blocks),
        out_specs=VMEM,
        out_shape=jax.ShapeDtypeStruct((weights.shape[0], rank), F32),
        scratch_shapes=[pltpu.VMEM(weights.shape, BF16), pltpu.SemaphoreType.DMA],
        compiler_params=params(),
    )(ids, weights, *blocks)


def coefficients(ids, members, weights, first, near, far, blocks):
    hidden = weights.shape[0]
    rank, rows = blocks[0].shape
    return pl.pallas_call(
        coef_kernel,
        in_specs=[SMEM, SMEM, HBM] + [VMEM] * (len(blocks) + 3),
        out_specs=HBM,
        out_shape=jax.ShapeDtypeStruct((hidden, rank), BF16),
        scratch_shapes=[
            pltpu.VMEM((hidden, len(blocks) * rows), BF16),
            pltpu.VMEM((hidden, rank), BF16),
            pltpu.SemaphoreType.DMA,
            pltpu.SemaphoreType.DMA,
        ],
        compiler_params=params(),
    )(ids, members, weights, first, near, far, *blocks)


def swap(block, distance):
    count = lax.axis_size("expert")
    return lax.ppermute(block, "expert", [(i, i ^ distance) for i in range(count)])


def tied(value, values, keys):
    value, *others = lax.optimization_barrier((value, *[values[k] for k in keys]))
    values.update(zip(keys, others))
    return value


def halves(keep, other):
    cut = keep.shape[0] // 2
    return keep[:cut] + other[:cut], keep[cut:] + other[cut:]


def local(down_proj, cov_factor, sketch, membership):
    devices = lax.axis_size("expert")
    weights = down_proj[0]
    width = weights.shape[1]
    last = devices.bit_length() - 2
    half, quarter = devices // 2, devices // 4
    me = lax.axis_index("expert")
    ids = me.astype(jnp.int32).reshape(1)

    blocks = partial_blocks(ids, cov_factor[0], sketch[0], weights, devices)
    order = [half]
    for s in range(1, half):
        order += [half + s, s]
    got = {0: blocks[0]}
    for k, s in enumerate(order):
        block = blocks[s]
        if k >= AHEAD:
            block = tied(block, got, order[k - AHEAD : k - AHEAD + 1])
        got[s] = swap(block, s)

    rows_t, keep, send, blocks = cluster_sums(ids, membership, [got[s] for s in range(devices)])

    crossing, inner = list(range(half, devices)), list(range(1, half))
    values = {0: blocks[0]}
    unit = max(1, devices // 16)

    def start(across, within, gate):
        keys = []
        for queue, count in ((crossing, across), (inner, within)):
            for _ in range(min(count * unit, len(queue))):
                s = queue.pop(0)
                block = blocks[s]
                if gate is not None:
                    block, gate = lax.optimization_barrier((block, gate))
                values[s] = swap(block, s)
                keys.append(s)
        return keys, gate

    other = swap(send, 1)
    waiting, _ = start(1, 1, None)
    for bit in range(1, last):
        keep, send = halves(keep, other)
        if bit > 1:
            send = tied(send, values, waiting)
            waiting, send = start(*PLAN["sum"], send)
        other = swap(send, 1 << bit)
    gram = tied(keep + other, values, waiting)
    waiting, gram = start(*PLAN["last"], gram)
    gram = gram + swap(gram, half)
    gram = tied(gram, values, waiting)
    waiting, gram = start(*PLAN["invert"], gram)
    inverse, rows = inverse_factor(gram[0], rows_t, math.sqrt(width))
    near = tied(inverse[None], values, waiting)
    for bit in reversed(range(1, last)):
        waiting, near = start(*PLAN["share"], near)
        near = jnp.concatenate([near, swap(near, 1 << bit)], axis=0)
        near = tied(near, values, waiting)
    far = swap(near, 1)
    start(devices, devices, near)

    first = first_product(ids, weights, [values[s] for s in range(half + quarter)])
    basis = basis_rows(ids, rows, near, far)
    coef = coefficients(
        ids, membership, weights, first, near, far, [values[s] for s in range(half + quarter, devices)]
    )
    return (coef[None], basis)


def solution(mesh):
    placed = (
        P(("groups", "expert"), None, None),
        P(("groups", "expert"), None, None),
        P(("groups", "expert"), None, None),
        P("groups"),
    )
    return jax.shard_map(
        local,
        mesh=mesh,
        in_specs=placed,
        out_specs=(P(("groups", "expert"), None, None), P("groups", "expert", None)),
        check_vma=False,
    )
```

```python
import functools
import math

import jax
import jax.numpy as jnp
from jax import lax
from jax.experimental import pallas as pl
from jax.experimental.pallas import tpu as pltpu
from jax.sharding import PartitionSpec as P

F32 = jnp.float32
BF16 = jnp.bfloat16
MIB = 1024 * 1024
PANEL = 8
BLOCK = 64
BUSY = {"invert": 40, "basis": 0, "product": 0, "late": 1}
VMEM = pl.BlockSpec(memory_space=pltpu.VMEM)
SMEM = pl.BlockSpec(memory_space=pltpu.SMEM)
HBM = pl.BlockSpec(memory_space=pltpu.MemorySpace.HBM)


def dot(a, b, dims):
    return lax.dot_general(a, b, (dims, ((), ())), preferred_element_type=F32)


def busy(microseconds):
    return pl.CostEstimate(flops=0, bytes_accessed=int(3.5e6 * microseconds), transcendentals=0)


def params(mib=24):
    return pltpu.CompilerParams(vmem_limit_bytes=mib * MIB)


def base_cluster(me, devices):
    last = devices.bit_length() - 2
    return sum(((me >> s) & 1) << (last - 1 - s) for s in range(last))


def weight_copies(me, weights_hbm, weights, sems, rows, half, far):
    quarter = half // 2
    columns = quarter * rows
    own = me // half
    first = (1 - own if far else own) * 2
    copies = []
    for part in range(2):
        start = (first + (me % half // quarter ^ part)) * columns
        copies.append(
            pltpu.make_async_copy(
                weights_hbm.at[:, pl.ds(pl.multiple_of(start, columns), columns)],
                weights.at[part],
                sems.at[part],
            )
        )
    return copies


def slot_blocks(me, weighted, weights, copy, part, product, outs):
    count = product.shape[0]
    rows = product.shape[2]
    copy.wait()
    wide = dot(weighted, weights[part], ((1,), (0,))).astype(BF16)
    for b in range(count):
        product[b] = wide[:, b * rows : (b + 1) * rows]
    for t in range(count):
        outs[(part * count + t) // 2][t % 2] = product[me % count ^ t]


def far_partial_kernel(half, ids_ref, cov_hbm, sketch_hbm, weights_hbm, *refs):
    *outs, weighted_ref = refs[: half // 2 + 1]
    cov, sketch, weights, product, in_sems, sems = refs[half // 2 + 1 :]
    me = ids_ref[0]
    cov_copy = pltpu.make_async_copy(cov_hbm, cov, in_sems.at[0])
    sketch_copy = pltpu.make_async_copy(sketch_hbm, sketch, in_sems.at[1])
    copies = weight_copies(me, weights_hbm, weights, sems, product.shape[2], half, True)
    cov_copy.start()
    sketch_copy.start()
    copies[0].start()
    cov_copy.wait()
    sketch_copy.wait()
    copies[1].start()
    weighted = dot(sketch[...], cov[...], ((0,), (1,))).astype(BF16)
    weighted_ref[...] = weighted
    for part in range(2):
        slot_blocks(me, weighted, weights, copies[part], part, product, outs)


def near_partial_kernel(half, ids_ref, weighted_ref, weights_hbm, *refs):
    *outs, weights, product, sems = refs
    me = ids_ref[0]
    copies = weight_copies(me, weights_hbm, weights, sems, product.shape[2], half, False)
    for copy in copies:
        copy.start()
    for part in range(2):
        slot_blocks(me, weighted_ref[...], weights, copies[part], part, product, outs)


def partial_blocks(ids, cov, sketch, weights, devices):
    hidden, width = weights.shape
    rank = sketch.shape[1]
    rows = width // devices
    half = devices // 2
    pair = jax.ShapeDtypeStruct((2, rank, rows), BF16)
    scratch = [
        pltpu.VMEM((2, hidden, width // 4), BF16),
        pltpu.VMEM((half // 2, rank, rows), BF16),
    ]
    sems = pltpu.SemaphoreType.DMA((2,))
    *far, weighted = pl.pallas_call(
        functools.partial(far_partial_kernel, half),
        in_specs=[SMEM, HBM, HBM, HBM],
        out_specs=[VMEM] * (half // 2 + 1),
        out_shape=[pair] * (half // 2) + [jax.ShapeDtypeStruct((rank, hidden), BF16)],
        scratch_shapes=[pltpu.VMEM(cov.shape, BF16), pltpu.VMEM(sketch.shape, BF16)]
        + scratch
        + [sems, sems],
        compiler_params=params(62),
    )(ids, cov, sketch, weights)
    near = pl.pallas_call(
        functools.partial(near_partial_kernel, half),
        in_specs=[SMEM, VMEM, HBM],
        out_specs=[VMEM] * (half // 2),
        out_shape=[pair] * (half // 2),
        scratch_shapes=scratch + [sems],
        compiler_params=params(),
    )(ids, weighted, weights)
    return [*near, *far]


def cluster_kernel(pairs, ids_ref, member_ref, *refs):
    received, passed, refs = refs[:pairs], refs[pairs : 2 * pairs], refs[2 * pairs :]
    rows_ref, keep_ref, send_ref = refs[:3]
    outs, total = refs[3 : 3 + pairs], refs[-1]
    me = ids_ref[0]
    base = base_cluster(me, 2 * pairs)
    half = rows_ref.shape[1] // 2
    total[...] = jnp.zeros_like(total)
    for q in range(pairs):
        for i, ref in enumerate((received[q], passed[q])):
            c = member_ref[me ^ (2 * q + i)]
            total[c] = total[c] + ref[i].astype(F32)
    rows_ref[...] = total[...].astype(BF16)
    for q in range(pairs):
        for i in range(2):
            outs[q][i] = rows_ref[member_ref[me ^ (2 * q + i)]]
    kept = keep_ref.shape[0]

    @pl.loop(0, kept)
    def _(k):
        for out_ref, slot in ((send_ref, k + kept), (keep_ref, k)):
            block = rows_ref[base ^ slot]
            full = dot(block, block, ((1,), (1,)))
            out_ref[k, 0] = full[:half, :half]
            out_ref[k, 1] = full[half:, :half]
            out_ref[k, 2] = full[half:, half:]


def cluster_sums(ids, members, received, passed):
    pairs = len(received)
    _, rank, rows = received[0].shape
    gram = jax.ShapeDtypeStruct((pairs // 2, 3, rank // 2, rank // 2), F32)
    pair = jax.ShapeDtypeStruct((2, rank, rows), BF16)
    rows_t, keep, send, *outs = pl.pallas_call(
        functools.partial(cluster_kernel, pairs),
        in_specs=[SMEM, SMEM] + [VMEM] * (2 * pairs),
        out_specs=[VMEM] * (pairs + 3),
        out_shape=[jax.ShapeDtypeStruct((pairs, rank, rows), BF16), gram, gram] + [pair] * pairs,
        scratch_shapes=[pltpu.VMEM((pairs, rank, rows), F32)],
        compiler_params=params(),
    )(ids, members, *received, *passed)
    return rows_t, keep, send, outs


def stacked(x, axis, order):
    high = x.astype(BF16)
    rest = x - high.astype(F32)
    middle = rest.astype(BF16)
    low = (rest - middle.astype(F32)).astype(BF16)
    return jnp.concatenate([(high, middle, low)[i] for i in order], axis=axis)


def stack_left(x, axis):
    return stacked(x, axis, (0, 0, 1, 0, 2, 1))


def stack_right(x, axis):
    return stacked(x, axis, (0, 1, 0, 2, 0, 1))


def block_inverse(square):
    size = square.shape[0]
    lanes = 128
    groups = size // 8
    row = lax.broadcasted_iota(jnp.int32, (size, size), 0)
    col = lax.broadcasted_iota(jnp.int32, (size, size), 1)
    parts = [square, jnp.where(row == col, 1.0, 0.0)]
    if lanes > 2 * size:
        parts.append(jnp.zeros((size, lanes - 2 * size), F32))
    table = jnp.concatenate(parts, axis=1)
    tiles = [table[8 * g : 8 * g + 8, :] for g in range(groups)]
    sub = lax.broadcasted_iota(jnp.int32, (8, lanes), 0)
    pivots = [jnp.ones((8, lanes), F32) for _ in range(groups)]

    def spread(x):
        return jnp.broadcast_to(x, (8, lanes))

    for k in range(0, size, PANEL):
        first = k // 8
        columns = [
            [spread(tiles[g][:, k + i : k + i + 1]) for g in range(first, groups)]
            for i in range(PANEL)
        ]
        s = {}
        for m in range(PANEL):
            for i in range(m, PANEL):
                q = k + i
                s[m, i] = spread(columns[m][q // 8 - first][q % 8 : q % 8 + 1, :])
        rows = [spread(tiles[(k + i) // 8][(k + i) % 8 : (k + i) % 8 + 1, :]) for i in range(PANEL)]
        inverse = []
        for m in range(PANEL):
            inverse.append(1.0 / s[m, m])
            for i in range(m + 1, PANEL):
                factor = s[m, i] * inverse[m]
                for t in range(i, PANEL):
                    s[i, t] = s[i, t] - factor * s[m, t]
                rows[i] = rows[i] - factor * rows[m]
        factors = []
        for m in range(PANEL):
            column = []
            for g in range(groups - first):
                x = columns[m][g]
                for t in range(m):
                    x = x - factors[t][g] * s[t, m]
                column.append(x * inverse[m])
            factors.append(column)
        for g in range(first, groups):
            tile = tiles[g]
            for m in range(PANEL):
                x = factors[m][g - first]
                if 8 * g <= k + m:
                    x = jnp.where(sub + 8 * g > k + m, x, 0.0)
                tile = tile - x * rows[m]
            tiles[g] = tile
        for m in range(PANEL):
            q = k + m
            pivots[q // 8] = jnp.where(sub == q % 8, s[m, m], pivots[q // 8])
    out = [tiles[g] * lax.rsqrt(pivots[g]) for g in range(groups)]
    return jnp.concatenate(out, axis=0)[:, size : 2 * size]


def invert(work):
    n = work.shape[0]
    for top in range(0, n, BLOCK):
        left = top // 128 * 128
        bottom = top + BLOCK
        square = work[top:bottom, left : left + 128][:, top - left : bottom - left]
        scaled = dot(
            stack_left(block_inverse(square), 1), stack_right(work[top:bottom, :], 0), ((1,), (0,))
        )
        work[top:bottom, n:] = scaled[:, n:]
        if bottom < n:
            start = bottom // 128 * 128
            change = dot(stack_left(scaled[:, start:n], 0), stack_right(scaled, 0), ((0,), (0,)))
            work[bottom:, :] = work[bottom:, :] - change[bottom - start :, :]


def identity(n):
    row = lax.broadcasted_iota(jnp.int32, (n, n), 0)
    col = lax.broadcasted_iota(jnp.int32, (n, n), 1)
    return jnp.where(row == col, 1.0, 0.0)


def inverse_kernel(scale, gram_ref, rows_t_ref, out_ref, rows_ref, work):
    for c in range(rows_ref.shape[0]):
        rows_ref[c] = rows_t_ref[c].T
    half = gram_ref.shape[1]
    n = 2 * half
    work[:half, :half] = gram_ref[0]
    work[half:, :half] = gram_ref[1]
    work[:half, half:n] = gram_ref[1].T
    work[half:, half:n] = gram_ref[2]
    work[:, n:] = identity(n)
    invert(work)
    out_ref[0] = (scale * work[:half, n : n + half]).astype(BF16)
    out_ref[1] = (scale * work[half:, n : n + half]).astype(BF16)
    out_ref[2] = (scale * work[half:, n + half :]).astype(BF16)


def inverse_factor(gram, rows_t, scale):
    half = gram.shape[1]
    clusters, rank, rows = rows_t.shape
    return pl.pallas_call(
        functools.partial(inverse_kernel, scale),
        in_specs=[VMEM] * 2,
        out_specs=[VMEM] * 2,
        out_shape=[
            jax.ShapeDtypeStruct(gram.shape, BF16),
            jax.ShapeDtypeStruct((clusters, rows, rank), BF16),
        ],
        scratch_shapes=[pltpu.VMEM((2 * half, 4 * half), F32)],
        compiler_params=params(),
        cost_estimate=busy(BUSY["invert"]),
    )(gram, rows_t)


def basis_kernel(ids_ref, rows_ref, near_ref, far_ref, out_hbm, out, sems):
    half = out.shape[2] // 2
    count = near_ref.shape[0]
    base = base_cluster(ids_ref[0], 4 * count)

    def copy(k):
        return pltpu.make_async_copy(out.at[k], out_hbm.at[base ^ k], sems.at[k])

    for k in range(2 * count):
        refs, i = (near_ref, k) if k < count else (far_ref, k - count)
        block = rows_ref[base ^ k]
        out[k, :, :half] = dot(block[:, :half], refs[i, 0], ((1,), (1,))).astype(BF16)
        out[k, :, half:] = (
            dot(block[:, :half], refs[i, 1], ((1,), (1,)))
            + dot(block[:, half:], refs[i, 2], ((1,), (1,)))
        ).astype(BF16)
        copy(k).start()
    for k in range(2 * count):
        copy(k).wait()


def basis_rows(ids, rows, near, far):
    return pl.pallas_call(
        basis_kernel,
        in_specs=[SMEM] + [VMEM] * 3,
        out_specs=HBM,
        out_shape=jax.ShapeDtypeStruct(rows.shape, BF16),
        scratch_shapes=[pltpu.VMEM(rows.shape, BF16), pltpu.SemaphoreType.DMA((rows.shape[0],))],
        compiler_params=params(),
        cost_estimate=busy(BUSY["basis"]),
    )(ids, rows, near, far)


def column_block(ref, index, rows):
    if rows % 128 == 0:
        return ref[:, pl.ds(pl.multiple_of(index * rows, rows), rows)]
    share = 128 // rows
    wide = ref[:, pl.ds(pl.multiple_of(index // share * 128, 128), 128)]
    block = wide[:, :rows]
    for i in range(1, share):
        block = jnp.where(index % share == i, wide[:, i * rows : (i + 1) * rows], block)
    return block


def slots_of(pairs):
    return [2 * q + i for q in pairs for i in range(2)]


def add_products(total, columns, refs, places):
    for column, (ref, block) in zip(columns, places):
        term = dot(column, refs[ref][block], ((1,), (1,)))
        total = term if total is None else total + term
    return total


def first_product_kernel(early, late, places, ids_ref, weights_hbm, *refs):
    *refs, out_ref, late_ref, weights, sem = refs
    me = ids_ref[0]
    rows = refs[0].shape[2]
    copy = pltpu.make_async_copy(weights_hbm, weights, sem)
    copy.start()
    copy.wait()
    columns = [column_block(weights, me ^ s, rows) for s in slots_of(early)]
    out_ref[...] = add_products(None, columns, refs, places)
    for k, s in enumerate(slots_of(late)):
        late_ref[:, k * rows : (k + 1) * rows] = column_block(weights, me ^ s, rows)


def late_product_kernel(places, weights_ref, first_ref, *refs):
    *refs, high_ref, low_ref = refs
    rows = refs[0].shape[2]
    columns = [weights_ref[:, k * rows : (k + 1) * rows] for k in range(len(places))]
    total = add_products(first_ref[...], columns, refs, places)
    high = total.astype(BF16)
    high_ref[...] = high
    low_ref[...] = (total - high.astype(F32)).astype(BF16)


def coef_kernel(ids_ref, member_ref, high_ref, low_ref, near_ref, far_ref, out_hbm, out, out_sem):
    me = ids_ref[0]
    slot = member_ref[me] ^ base_cluster(me, member_ref.shape[0])
    near = slot < near_ref.shape[0]
    inside = lax.rem(slot, near_ref.shape[0])
    half = out.shape[1] // 2

    def times(i, part):
        factor = jnp.where(near, near_ref[inside, i], far_ref[inside, i])
        high, low = high_ref[:, part], low_ref[:, part]
        return dot(high, factor, ((1,), (1,))) + dot(low, factor, ((1,), (1,)))

    left, right = slice(0, half), slice(half, 2 * half)
    out[:, left] = times(0, left).astype(BF16)
    out[:, right] = (times(1, left) + times(2, right)).astype(BF16)
    out_copy = pltpu.make_async_copy(out, out_hbm, out_sem)
    out_copy.start()
    out_copy.wait()


def first_product(ids, weights, early, late, arrays, places):
    hidden, width = weights.shape
    _, rank, rows = arrays[0].shape
    return pl.pallas_call(
        functools.partial(first_product_kernel, early, late, places),
        in_specs=[SMEM, HBM] + [VMEM] * len(arrays),
        out_specs=[VMEM] * 2,
        out_shape=[
            jax.ShapeDtypeStruct((hidden, rank), F32),
            jax.ShapeDtypeStruct((hidden, 2 * len(late) * rows), BF16),
        ],
        scratch_shapes=[pltpu.VMEM(weights.shape, BF16), pltpu.SemaphoreType.DMA],
        compiler_params=params(),
        cost_estimate=busy(BUSY["product"]),
    )(ids, weights, *arrays)


def late_product(late_weights, first, arrays, places):
    return pl.pallas_call(
        functools.partial(late_product_kernel, places),
        in_specs=[VMEM] * (len(arrays) + 2),
        out_specs=[VMEM] * 2,
        out_shape=[jax.ShapeDtypeStruct(first.shape, BF16)] * 2,
        compiler_params=params(),
        cost_estimate=busy(BUSY["late"]),
    )(late_weights, first, *arrays)


def coefficients(ids, members, product, near, far):
    out = product[0].shape
    return pl.pallas_call(
        coef_kernel,
        in_specs=[SMEM, SMEM] + [VMEM] * 4,
        out_specs=HBM,
        out_shape=jax.ShapeDtypeStruct(out, BF16),
        scratch_shapes=[pltpu.VMEM(out, BF16), pltpu.SemaphoreType.DMA],
        compiler_params=params(),
    )(ids, members, *product, near, far)


def swap(block, distance):
    count = lax.axis_size("expert")
    return lax.ppermute(block, "expert", [(i, i ^ distance) for i in range(count)])


def tied(value, values, keys):
    value, *others = lax.optimization_barrier((value, *[values[k] for k in keys]))
    values.update(zip(keys, others))
    return value


def halves(keep, other):
    cut = keep.shape[0] // 2
    return keep[:cut] + other[:cut], keep[cut:] + other[cut:]


def local(down_proj, cov_factor, sketch, membership):
    devices = lax.axis_size("expert")
    weights = down_proj[0]
    width = weights.shape[1]
    last = devices.bit_length() - 2
    half = devices // 2
    me = lax.axis_index("expert")
    ids = me.astype(jnp.int32).reshape(1)

    pairs = devices // 2
    middle = pairs // 2
    blocks = partial_blocks(ids, cov_factor[0], sketch[0], weights, devices)
    got = {0: blocks[0]}
    far = list(range(middle, pairs))
    near = list(range(1, middle))
    share = -(-len(near) // max(1, len(far) - 2))
    for q in far[:2] + near:
        got[q] = swap(blocks[q], 2 * q)
    for k, q in enumerate(far[2:]):
        block = tied(blocks[q], got, [far[k]] + near[k * share : (k + 1) * share])
        got[q] = swap(block, 2 * q)
    every = range(pairs)
    rows_t, keep, send, blocks = cluster_sums(
        ids, membership, [got[q] for q in every], [swap(got[q], 1) for q in every]
    )

    even = [q for q in range(pairs - 1, middle - 1, -1) if q % 2 == 0]
    last_pairs = [q for q in range(middle, pairs) if q % 2]
    inner = list(range(1, middle))
    inner_parts = [q for q in inner if q % 2 == 0], [q for q in inner if q % 4 == 1], [q for q in inner if q % 4 == 3]
    values = {0: blocks[0]}
    passed = {}

    def start(keys, gate):
        for q in keys:
            block, gate = lax.optimization_barrier((blocks[q], gate))
            values[q] = swap(block, 2 * q)
        return gate

    def pass_on(keys):
        pair = values[keys[0]] if len(keys) == 1 else jnp.concatenate([values[q] for q in keys])
        passed[tuple(keys)] = swap(pair, 1)

    def blocks_for(keys):
        groups = [g for g in passed if set(g) <= set(keys)]
        arrays = [values[q] for q in keys] + [passed[g] for g in groups]
        places = []
        for k, q in enumerate(keys):
            (n, g), = ((n, g) for n, g in enumerate(groups) if q in g)
            places += [(k, 0), (len(keys) + n, 2 * g.index(q) + 1)]
        return arrays, places

    cut = len(even) // 2
    send = start(even[:cut] + inner_parts[0], send)
    send = start(even[cut:], send)
    other = swap(send, 1)
    for bit in range(1, last):
        keep, send = halves(keep, other)
        if bit == 2:
            send = tied(send, values, even[:cut] + inner_parts[0])
            send = start(inner_parts[1] + inner_parts[2], send)
        other = swap(send, 1 << bit)
    gram = tied(keep + other, values, even[cut:] + inner_parts[1])
    gram = gram + swap(gram, half)
    gram = tied(gram, values, inner_parts[2])

    cut = len(last_pairs) // 2
    gram = start(last_pairs[:cut], gram)
    early = [q for q in every if q not in last_pairs]
    for q in early:
        if (q,) not in passed:
            values[q], gram = lax.optimization_barrier((values[q], gram))
            pass_on([q])
    inverse, rows = inverse_factor(gram[0], rows_t, math.sqrt(width))
    near = tied(inverse[None], passed, list(passed))
    first, late_weights = first_product(ids, weights, early, last_pairs, *blocks_for(early))
    near = start(last_pairs[cut:], near)
    pieces = [near]
    for bit in reversed(range(1, last)):
        if len(pieces) > 2:
            pieces = [jnp.concatenate(pieces, axis=0)]
        pieces += [swap(piece, 1 << bit) for piece in pieces]
        if bit == last - 1:
            pieces[1] = tied(pieces[1], values, last_pairs[:cut])
    near = jnp.concatenate(pieces, axis=0)
    near, first = lax.optimization_barrier((near, first))
    near = tied(near, values, last_pairs[cut:])
    for q in last_pairs:
        pass_on([q])
    far = swap(near, 1)
    product = late_product(late_weights, first, *blocks_for(last_pairs))
    basis = basis_rows(ids, rows, near, far)
    coef = coefficients(ids, membership, product, near, far)
    return (coef[None], basis)


def solution(mesh):
    placed = (
        P(("groups", "expert"), None, None),
        P(("groups", "expert"), None, None),
        P(("groups", "expert"), None, None),
        P("groups"),
    )
    return jax.shard_map(
        local,
        mesh=mesh,
        in_specs=placed,
        out_specs=(P(("groups", "expert"), None, None), P("groups", "expert", None)),
        check_vma=False,
    )
```

```python
import functools
import math

import jax
import jax.numpy as jnp
from jax import lax
from jax.experimental import pallas as pl
from jax.experimental.pallas import tpu as pltpu
from jax.sharding import PartitionSpec as P

F32 = jnp.float32
BF16 = jnp.bfloat16
MIB = 1024 * 1024
PANEL = 8
BLOCK = 64
BUSY = {"invert": 40, "basis": 2, "product": 0, "late": 1}
VMEM = pl.BlockSpec(memory_space=pltpu.VMEM)
SMEM = pl.BlockSpec(memory_space=pltpu.SMEM)
HBM = pl.BlockSpec(memory_space=pltpu.MemorySpace.HBM)


def dot(a, b, dims):
    return lax.dot_general(a, b, (dims, ((), ())), preferred_element_type=F32)


def busy(microseconds):
    return pl.CostEstimate(flops=0, bytes_accessed=int(3.5e6 * microseconds), transcendentals=0)


def params(mib=24):
    return pltpu.CompilerParams(vmem_limit_bytes=mib * MIB)


def base_cluster(me, devices):
    last = devices.bit_length() - 2
    return sum(((me >> s) & 1) << (last - 1 - s) for s in range(last))


def weight_copies(me, weights_hbm, weights, sems, rows, half, far):
    quarter = half // 2
    columns = quarter * rows
    own = me // half
    first = (1 - own if far else own) * 2
    copies = []
    for part in range(2):
        start = (first + (me % half // quarter ^ part)) * columns
        copies.append(
            pltpu.make_async_copy(
                weights_hbm.at[:, pl.ds(pl.multiple_of(start, columns), columns)],
                weights.at[part],
                sems.at[part],
            )
        )
    return copies


def slot_blocks(me, weighted, weights, copy, part, product, outs):
    count = product.shape[0]
    rows = product.shape[2]
    copy.wait()
    wide = dot(weighted, weights[part], ((1,), (0,))).astype(BF16)
    for b in range(count):
        product[b] = wide[:, b * rows : (b + 1) * rows]
    for t in range(count):
        outs[(part * count + t) // 2][t % 2] = product[me % count ^ t]


def far_partial_kernel(half, ids_ref, cov_hbm, sketch_hbm, weights_hbm, *refs):
    *outs, weighted_ref = refs[: half // 2 + 1]
    cov, sketch, weights, product, in_sems, sems = refs[half // 2 + 1 :]
    me = ids_ref[0]
    cov_copy = pltpu.make_async_copy(cov_hbm, cov, in_sems.at[0])
    sketch_copy = pltpu.make_async_copy(sketch_hbm, sketch, in_sems.at[1])
    copies = weight_copies(me, weights_hbm, weights, sems, product.shape[2], half, True)
    cov_copy.start()
    sketch_copy.start()
    copies[0].start()
    cov_copy.wait()
    sketch_copy.wait()
    copies[1].start()
    weighted = dot(sketch[...], cov[...], ((0,), (1,))).astype(BF16)
    weighted_ref[...] = weighted
    for part in range(2):
        slot_blocks(me, weighted, weights, copies[part], part, product, outs)


def near_partial_kernel(half, ids_ref, weighted_ref, weights_hbm, *refs):
    *outs, weights, product, sems = refs
    me = ids_ref[0]
    copies = weight_copies(me, weights_hbm, weights, sems, product.shape[2], half, False)
    for copy in copies:
        copy.start()
    for part in range(2):
        slot_blocks(me, weighted_ref[...], weights, copies[part], part, product, outs)


def partial_blocks(ids, cov, sketch, weights, devices):
    hidden, width = weights.shape
    rank = sketch.shape[1]
    rows = width // devices
    half = devices // 2
    pair = jax.ShapeDtypeStruct((2, rank, rows), BF16)
    scratch = [
        pltpu.VMEM((2, hidden, width // 4), BF16),
        pltpu.VMEM((half // 2, rank, rows), BF16),
    ]
    sems = pltpu.SemaphoreType.DMA((2,))
    *far, weighted = pl.pallas_call(
        functools.partial(far_partial_kernel, half),
        in_specs=[SMEM, HBM, HBM, HBM],
        out_specs=[VMEM] * (half // 2 + 1),
        out_shape=[pair] * (half // 2) + [jax.ShapeDtypeStruct((rank, hidden), BF16)],
        scratch_shapes=[pltpu.VMEM(cov.shape, BF16), pltpu.VMEM(sketch.shape, BF16)]
        + scratch
        + [sems, sems],
        compiler_params=params(62),
    )(ids, cov, sketch, weights)
    near = pl.pallas_call(
        functools.partial(near_partial_kernel, half),
        in_specs=[SMEM, VMEM, HBM],
        out_specs=[VMEM] * (half // 2),
        out_shape=[pair] * (half // 2),
        scratch_shapes=scratch + [sems],
        compiler_params=params(),
    )(ids, weighted, weights)
    return [*near, *far]


def cluster_kernel(pairs, ids_ref, member_ref, *refs):
    received, passed, refs = refs[:pairs], refs[pairs : 2 * pairs], refs[2 * pairs :]
    rows_ref, outs, total = refs[0], refs[1 : 1 + pairs], refs[-1]
    me = ids_ref[0]
    total[...] = jnp.zeros_like(total)
    for q in range(pairs):
        for i, ref in enumerate((received[q], passed[q])):
            c = member_ref[me ^ (2 * q + i)]
            total[c] = total[c] + ref[i].astype(F32)
    rows_ref[...] = total[...].astype(BF16)
    for q in range(pairs):
        for i in range(2):
            outs[q][i] = rows_ref[member_ref[me ^ (2 * q + i)]]


def gram_kernel(ids_ref, rows_ref, keep_ref, send_ref):
    half = rows_ref.shape[1] // 2
    kept = keep_ref.shape[0]
    base = base_cluster(ids_ref[0], 4 * kept)
    for k in range(kept):
        for out_ref, slot in ((send_ref, k + kept), (keep_ref, k)):
            block = rows_ref[base ^ slot]
            full = dot(block, block, ((1,), (1,)))
            out_ref[k, 0] = full[:half, :half]
            out_ref[k, 1] = full[half:, :half]
            out_ref[k, 2] = full[half:, half:]


def cluster_sums(ids, members, received, passed):
    pairs = len(received)
    _, rank, rows = received[0].shape
    gram = jax.ShapeDtypeStruct((pairs // 2, 3, rank // 2, rank // 2), F32)
    pair = jax.ShapeDtypeStruct((2, rank, rows), BF16)
    rows_t, *outs = pl.pallas_call(
        functools.partial(cluster_kernel, pairs),
        in_specs=[SMEM, SMEM] + [VMEM] * (2 * pairs),
        out_specs=[VMEM] * (pairs + 1),
        out_shape=[jax.ShapeDtypeStruct((pairs, rank, rows), BF16)] + [pair] * pairs,
        scratch_shapes=[pltpu.VMEM((pairs, rank, rows), F32)],
        compiler_params=params(),
    )(ids, members, *received, *passed)
    keep, send = pl.pallas_call(
        gram_kernel,
        in_specs=[SMEM, VMEM],
        out_specs=[VMEM] * 2,
        out_shape=[gram, gram],
        compiler_params=params(),
    )(ids, rows_t)
    return rows_t, keep, send, outs


def stacked(x, axis, order):
    high = x.astype(BF16)
    rest = x - high.astype(F32)
    middle = rest.astype(BF16)
    low = (rest - middle.astype(F32)).astype(BF16)
    return jnp.concatenate([(high, middle, low)[i] for i in order], axis=axis)


def stack_left(x, axis):
    return stacked(x, axis, (0, 0, 1, 0, 2, 1))


def stack_right(x, axis):
    return stacked(x, axis, (0, 1, 0, 2, 0, 1))


def block_inverse(square):
    size = square.shape[0]
    lanes = 128
    groups = size // 8
    row = lax.broadcasted_iota(jnp.int32, (size, size), 0)
    col = lax.broadcasted_iota(jnp.int32, (size, size), 1)
    parts = [square, jnp.where(row == col, 1.0, 0.0)]
    if lanes > 2 * size:
        parts.append(jnp.zeros((size, lanes - 2 * size), F32))
    table = jnp.concatenate(parts, axis=1)
    tiles = [table[8 * g : 8 * g + 8, :] for g in range(groups)]
    sub = lax.broadcasted_iota(jnp.int32, (8, lanes), 0)
    pivots = [jnp.ones((8, lanes), F32) for _ in range(groups)]

    def spread(x):
        return jnp.broadcast_to(x, (8, lanes))

    for k in range(0, size, PANEL):
        first = k // 8
        columns = [
            [spread(tiles[g][:, k + i : k + i + 1]) for g in range(first, groups)]
            for i in range(PANEL)
        ]
        s = {}
        for m in range(PANEL):
            for i in range(m, PANEL):
                q = k + i
                s[m, i] = spread(columns[m][q // 8 - first][q % 8 : q % 8 + 1, :])
        rows = [spread(tiles[(k + i) // 8][(k + i) % 8 : (k + i) % 8 + 1, :]) for i in range(PANEL)]
        inverse = []
        for m in range(PANEL):
            inverse.append(1.0 / s[m, m])
            for i in range(m + 1, PANEL):
                factor = s[m, i] * inverse[m]
                for t in range(i, PANEL):
                    s[i, t] = s[i, t] - factor * s[m, t]
                rows[i] = rows[i] - factor * rows[m]
        factors = []
        for m in range(PANEL):
            column = []
            for g in range(groups - first):
                x = columns[m][g]
                for t in range(m):
                    x = x - factors[t][g] * s[t, m]
                column.append(x * inverse[m])
            factors.append(column)
        for g in range(first, groups):
            tile = tiles[g]
            for m in range(PANEL):
                x = factors[m][g - first]
                if 8 * g <= k + m:
                    x = jnp.where(sub + 8 * g > k + m, x, 0.0)
                tile = tile - x * rows[m]
            tiles[g] = tile
        for m in range(PANEL):
            q = k + m
            pivots[q // 8] = jnp.where(sub == q % 8, s[m, m], pivots[q // 8])
    out = [tiles[g] * lax.rsqrt(pivots[g]) for g in range(groups)]
    return jnp.concatenate(out, axis=0)[:, size : 2 * size]


def invert(work):
    n = work.shape[0]
    for top in range(0, n, BLOCK):
        left = top // 128 * 128
        bottom = top + BLOCK
        square = work[top:bottom, left : left + 128][:, top - left : bottom - left]
        scaled = dot(
            stack_left(block_inverse(square), 1), stack_right(work[top:bottom, :], 0), ((1,), (0,))
        )
        work[top:bottom, n:] = scaled[:, n:]
        if bottom < n:
            start = bottom // 128 * 128
            change = dot(stack_left(scaled[:, start:n], 0), stack_right(scaled, 0), ((0,), (0,)))
            work[bottom:, :] = work[bottom:, :] - change[bottom - start :, :]


def identity(n):
    row = lax.broadcasted_iota(jnp.int32, (n, n), 0)
    col = lax.broadcasted_iota(jnp.int32, (n, n), 1)
    return jnp.where(row == col, 1.0, 0.0)


def inverse_kernel(scale, gram_ref, rows_t_ref, out_ref, rows_ref, work):
    for c in range(rows_ref.shape[0]):
        rows_ref[c] = rows_t_ref[c].T
    half = gram_ref.shape[1]
    n = 2 * half
    work[:half, :half] = gram_ref[0]
    work[half:, :half] = gram_ref[1]
    work[:half, half:n] = gram_ref[1].T
    work[half:, half:n] = gram_ref[2]
    work[:, n:] = identity(n)
    invert(work)
    out_ref[0] = (scale * work[:half, n : n + half]).astype(BF16)
    out_ref[1] = (scale * work[half:, n : n + half]).astype(BF16)
    out_ref[2] = (scale * work[half:, n + half :]).astype(BF16)


def inverse_factor(gram, rows_t, scale):
    half = gram.shape[1]
    clusters, rank, rows = rows_t.shape
    return pl.pallas_call(
        functools.partial(inverse_kernel, scale),
        in_specs=[VMEM] * 2,
        out_specs=[VMEM] * 2,
        out_shape=[
            jax.ShapeDtypeStruct(gram.shape, BF16),
            jax.ShapeDtypeStruct((clusters, rows, rank), BF16),
        ],
        scratch_shapes=[pltpu.VMEM((2 * half, 4 * half), F32)],
        compiler_params=params(),
        cost_estimate=busy(BUSY["invert"]),
    )(gram, rows_t)


def basis_kernel(ids_ref, rows_ref, near_ref, far_ref, out_hbm, out, sems):
    half = out.shape[2] // 2
    count = near_ref.shape[0]
    base = base_cluster(ids_ref[0], 4 * count)

    def copy(k):
        return pltpu.make_async_copy(out.at[k], out_hbm.at[base ^ k], sems.at[k])

    for k in range(2 * count):
        refs, i = (near_ref, k) if k < count else (far_ref, k - count)
        block = rows_ref[base ^ k]
        out[k, :, :half] = dot(block[:, :half], refs[i, 0], ((1,), (1,))).astype(BF16)
        out[k, :, half:] = (
            dot(block[:, :half], refs[i, 1], ((1,), (1,)))
            + dot(block[:, half:], refs[i, 2], ((1,), (1,)))
        ).astype(BF16)
        copy(k).start()
    for k in range(2 * count):
        copy(k).wait()


def basis_rows(ids, rows, near, far):
    return pl.pallas_call(
        basis_kernel,
        in_specs=[SMEM] + [VMEM] * 3,
        out_specs=HBM,
        out_shape=jax.ShapeDtypeStruct(rows.shape, BF16),
        scratch_shapes=[pltpu.VMEM(rows.shape, BF16), pltpu.SemaphoreType.DMA((rows.shape[0],))],
        compiler_params=params(),
        cost_estimate=busy(BUSY["basis"]),
    )(ids, rows, near, far)


def column_block(ref, index, rows):
    if rows % 128 == 0:
        return ref[:, pl.ds(pl.multiple_of(index * rows, rows), rows)]
    share = 128 // rows
    wide = ref[:, pl.ds(pl.multiple_of(index // share * 128, 128), 128)]
    block = wide[:, :rows]
    for i in range(1, share):
        block = jnp.where(index % share == i, wide[:, i * rows : (i + 1) * rows], block)
    return block


def slots_of(pairs):
    return [2 * q + i for q in pairs for i in range(2)]


def add_products(total, columns, refs, places):
    for column, (ref, block) in zip(columns, places):
        term = dot(column, refs[ref][block], ((1,), (1,)))
        total = term if total is None else total + term
    return total


def first_product_kernel(early, late, places, ids_ref, weights_hbm, *refs):
    *refs, out_ref, late_ref, weights, sem = refs
    me = ids_ref[0]
    rows = refs[0].shape[2]
    copy = pltpu.make_async_copy(weights_hbm, weights, sem)
    copy.start()
    copy.wait()
    columns = [column_block(weights, me ^ s, rows) for s in slots_of(early)]
    out_ref[...] = add_products(None, columns, refs, places)
    for k, s in enumerate(slots_of(late)):
        late_ref[:, k * rows : (k + 1) * rows] = column_block(weights, me ^ s, rows)


def late_product_kernel(places, weights_ref, first_ref, *refs):
    *refs, high_ref, low_ref = refs
    rows = refs[0].shape[2]
    columns = [weights_ref[:, k * rows : (k + 1) * rows] for k in range(len(places))]
    total = add_products(first_ref[...], columns, refs, places)
    high = total.astype(BF16)
    high_ref[...] = high
    low_ref[...] = (total - high.astype(F32)).astype(BF16)


def coef_kernel(ids_ref, member_ref, high_ref, low_ref, near_ref, far_ref, out_hbm, out, out_sem):
    me = ids_ref[0]
    slot = member_ref[me] ^ base_cluster(me, member_ref.shape[0])
    near = slot < near_ref.shape[0]
    inside = lax.rem(slot, near_ref.shape[0])
    half = out.shape[1] // 2

    def times(i, part):
        factor = jnp.where(near, near_ref[inside, i], far_ref[inside, i])
        high, low = high_ref[:, part], low_ref[:, part]
        return dot(high, factor, ((1,), (1,))) + dot(low, factor, ((1,), (1,)))

    left, right = slice(0, half), slice(half, 2 * half)
    out[:, left] = times(0, left).astype(BF16)
    out[:, right] = (times(1, left) + times(2, right)).astype(BF16)
    out_copy = pltpu.make_async_copy(out, out_hbm, out_sem)
    out_copy.start()
    out_copy.wait()


def first_product(ids, weights, early, late, arrays, places):
    hidden, width = weights.shape
    _, rank, rows = arrays[0].shape
    return pl.pallas_call(
        functools.partial(first_product_kernel, early, late, places),
        in_specs=[SMEM, HBM] + [VMEM] * len(arrays),
        out_specs=[VMEM] * 2,
        out_shape=[
            jax.ShapeDtypeStruct((hidden, rank), F32),
            jax.ShapeDtypeStruct((hidden, 2 * len(late) * rows), BF16),
        ],
        scratch_shapes=[pltpu.VMEM(weights.shape, BF16), pltpu.SemaphoreType.DMA],
        compiler_params=params(),
        cost_estimate=busy(BUSY["product"]),
    )(ids, weights, *arrays)


def late_product(late_weights, first, arrays, places):
    return pl.pallas_call(
        functools.partial(late_product_kernel, places),
        in_specs=[VMEM] * (len(arrays) + 2),
        out_specs=[VMEM] * 2,
        out_shape=[jax.ShapeDtypeStruct(first.shape, BF16)] * 2,
        compiler_params=params(),
        cost_estimate=busy(BUSY["late"]),
    )(late_weights, first, *arrays)


def coefficients(ids, members, product, near, far):
    out = product[0].shape
    return pl.pallas_call(
        coef_kernel,
        in_specs=[SMEM, SMEM] + [VMEM] * 4,
        out_specs=HBM,
        out_shape=jax.ShapeDtypeStruct(out, BF16),
        scratch_shapes=[pltpu.VMEM(out, BF16), pltpu.SemaphoreType.DMA],
        compiler_params=params(),
    )(ids, members, *product, near, far)


def swap(block, distance):
    count = lax.axis_size("expert")
    return lax.ppermute(block, "expert", [(i, i ^ distance) for i in range(count)])


def tied(value, values, keys):
    value, *others = lax.optimization_barrier((value, *[values[k] for k in keys]))
    values.update(zip(keys, others))
    return value


def halves(keep, other):
    cut = keep.shape[0] // 2
    first, second = other if isinstance(other, tuple) else (other[:cut], other[cut:])
    return keep[:cut] + first, keep[cut:] + second


def local(down_proj, cov_factor, sketch, membership):
    devices = lax.axis_size("expert")
    weights = down_proj[0]
    width = weights.shape[1]
    last = devices.bit_length() - 2
    half = devices // 2
    me = lax.axis_index("expert")
    ids = me.astype(jnp.int32).reshape(1)

    pairs = devices // 2
    middle = pairs // 2
    blocks = partial_blocks(ids, cov_factor[0], sketch[0], weights, devices)
    got = {0: blocks[0]}
    far = list(range(middle, pairs))
    near = list(range(1, middle))
    share = -(-len(near) // max(1, len(far) - 2))
    for q in far[:2] + near:
        got[q] = swap(blocks[q], 2 * q)
    for k, q in enumerate(far[2:]):
        block = tied(blocks[q], got, [far[k]] + near[k * share : (k + 1) * share])
        got[q] = swap(block, 2 * q)
    every = range(pairs)
    rows_t, keep, send, blocks = cluster_sums(
        ids, membership, [got[q] for q in every], [swap(got[q], 1) for q in every]
    )

    even = [q for q in range(pairs - 1, middle - 1, -1) if q % 2 == 0]
    last_pairs = [q for q in range(middle, pairs) if q % 2]
    inner = list(range(1, middle))
    inner_parts = [q for q in inner if q % 2 == 0], [q for q in inner if q % 4 == 1], [q for q in inner if q % 4 == 3]
    values = {0: blocks[0]}
    passed = {}

    def start(keys, gate):
        for q in keys:
            block, gate = lax.optimization_barrier((blocks[q], gate))
            values[q] = swap(block, 2 * q)
        return gate

    def pass_on(keys):
        pair = values[keys[0]] if len(keys) == 1 else jnp.concatenate([values[q] for q in keys])
        passed[tuple(keys)] = swap(pair, 1)

    def blocks_for(keys):
        groups = [g for g in passed if set(g) <= set(keys)]
        arrays = [values[q] for q in keys] + [passed[g] for g in groups]
        places = []
        for k, q in enumerate(keys):
            (n, g), = ((n, g) for n, g in enumerate(groups) if q in g)
            places += [(k, 0), (len(keys) + n, 2 * g.index(q) + 1)]
        return arrays, places

    share = len(even) // 2
    rows_t = start(inner_parts[0] + even, rows_t)
    other = swap(send, 1)
    for bit in range(1, last):
        keep, send = halves(keep, other)
        if bit == 2:
            for q in even[:share]:
                pass_on([q])
            send = tied(send, values, inner_parts[0])
            send = tied(send, passed, [(q,) for q in even[:share]])
            send = start(inner_parts[1] + inner_parts[2], send)
        if bit == 1 and last > 2:
            cut = send.shape[0] // 2
            other = swap(send[:cut], 1 << bit), swap(send[cut:], 1 << bit)
        else:
            other = swap(send, 1 << bit)
    gram = tied(keep + other, values, even[share:] + inner_parts[1])
    gram = gram + swap(gram, half)
    gram = tied(gram, values, inner_parts[2])

    cut = len(last_pairs) // 2
    early = [q for q in every if q not in last_pairs]
    for q in early:
        if (q,) not in passed:
            values[q], gram = lax.optimization_barrier((values[q], gram))
            pass_on([q])
    gram = start(last_pairs[:cut], gram)
    inverse, rows = inverse_factor(gram[0], rows_t, math.sqrt(width))
    near = tied(inverse[None], passed, list(passed))
    first, late_weights = first_product(ids, weights, early, last_pairs, *blocks_for(early))
    near = start(last_pairs[cut:], near)
    pieces = [near]
    for bit in reversed(range(1, last)):
        if len(pieces) > 2:
            pieces = [jnp.concatenate(pieces, axis=0)]
        pieces += [swap(piece, 1 << bit) for piece in pieces]
        if bit == last - 1:
            pieces[1] = tied(pieces[1], values, last_pairs[:cut])
            pieces[1], first = lax.optimization_barrier((pieces[1], first))
    far = jnp.concatenate([swap(piece, 1) for piece in pieces], axis=0)
    near = jnp.concatenate(pieces, axis=0)
    for q in last_pairs:
        pass_on([q])
    near, far = lax.optimization_barrier((near, far))
    basis = basis_rows(ids, rows, near, far)
    near = tied(near, passed, [(q,) for q in last_pairs[cut:]])
    product = late_product(late_weights, first, *blocks_for(last_pairs))
    coef = coefficients(ids, membership, product, near, far)
    return (coef[None], basis)


def solution(mesh):
    placed = (
        P(("groups", "expert"), None, None),
        P(("groups", "expert"), None, None),
        P(("groups", "expert"), None, None),
        P("groups"),
    )
    return jax.shard_map(
        local,
        mesh=mesh,
        in_specs=placed,
        out_specs=(P(("groups", "expert"), None, None), P("groups", "expert", None)),
        check_vma=False,
    )
```

```python
import functools
import math

import jax
import jax.numpy as jnp
from jax import lax
from jax.experimental import pallas as pl
from jax.experimental.pallas import tpu as pltpu
from jax.sharding import PartitionSpec as P

F32 = jnp.float32
BF16 = jnp.bfloat16
MIB = 1024 * 1024
PANEL = 8
BLOCK = 64
BUSY = {"invert": 40, "basis": 2, "product": 0, "late": 1}
VMEM = pl.BlockSpec(memory_space=pltpu.VMEM)
SMEM = pl.BlockSpec(memory_space=pltpu.SMEM)
HBM = pl.BlockSpec(memory_space=pltpu.MemorySpace.HBM)


def dot(a, b, dims):
    return lax.dot_general(a, b, (dims, ((), ())), preferred_element_type=F32)


def busy(microseconds):
    return pl.CostEstimate(flops=0, bytes_accessed=int(3.5e6 * microseconds), transcendentals=0)


def params(mib=24):
    return pltpu.CompilerParams(vmem_limit_bytes=mib * MIB)


def base_cluster(me, devices):
    last = devices.bit_length() - 2
    return sum(((me >> s) & 1) << (last - 1 - s) for s in range(last))


def weight_copies(me, weights_hbm, weights, sems, rows, half, far):
    quarter = half // 2
    columns = quarter * rows
    own = me // half
    first = (1 - own if far else own) * 2
    copies = []
    for part in range(2):
        start = (first + (me % half // quarter ^ part)) * columns
        copies.append(
            pltpu.make_async_copy(
                weights_hbm.at[:, pl.ds(pl.multiple_of(start, columns), columns)],
                weights.at[part],
                sems.at[part],
            )
        )
    return copies


def slot_blocks(me, weighted, weights, copy, part, product, outs):
    count = product.shape[0]
    rows = product.shape[2]
    copy.wait()
    wide = dot(weighted, weights[part], ((1,), (0,))).astype(BF16)
    for b in range(count):
        product[b] = wide[:, b * rows : (b + 1) * rows]
    for t in range(count):
        outs[(part * count + t) // 2][t % 2] = product[me % count ^ t]


def far_partial_kernel(half, ids_ref, cov_hbm, sketch_hbm, weights_hbm, *refs):
    *outs, weighted_ref = refs[: half // 2 + 1]
    cov, sketch, weights, product, in_sems, sems = refs[half // 2 + 1 :]
    me = ids_ref[0]
    cov_copy = pltpu.make_async_copy(cov_hbm, cov, in_sems.at[0])
    sketch_copy = pltpu.make_async_copy(sketch_hbm, sketch, in_sems.at[1])
    copies = weight_copies(me, weights_hbm, weights, sems, product.shape[2], half, True)
    cov_copy.start()
    sketch_copy.start()
    copies[0].start()
    copies[1].start()
    cov_copy.wait()
    sketch_copy.wait()
    weighted = dot(sketch[...], cov[...], ((0,), (1,))).astype(BF16)
    weighted_ref[...] = weighted
    for part in range(2):
        slot_blocks(me, weighted, weights, copies[part], part, product, outs)


def near_partial_kernel(half, ids_ref, weighted_ref, weights_hbm, *refs):
    *outs, weights, product, sems = refs
    me = ids_ref[0]
    copies = weight_copies(me, weights_hbm, weights, sems, product.shape[2], half, False)
    for copy in copies:
        copy.start()
    for part in range(2):
        slot_blocks(me, weighted_ref[...], weights, copies[part], part, product, outs)


def partial_blocks(ids, cov, sketch, weights, devices):
    hidden, width = weights.shape
    rank = sketch.shape[1]
    rows = width // devices
    half = devices // 2
    pair = jax.ShapeDtypeStruct((2, rank, rows), BF16)
    scratch = [
        pltpu.VMEM((2, hidden, width // 4), BF16),
        pltpu.VMEM((half // 2, rank, rows), BF16),
    ]
    sems = pltpu.SemaphoreType.DMA((2,))
    *far, weighted = pl.pallas_call(
        functools.partial(far_partial_kernel, half),
        in_specs=[SMEM, HBM, HBM, HBM],
        out_specs=[VMEM] * (half // 2 + 1),
        out_shape=[pair] * (half // 2) + [jax.ShapeDtypeStruct((rank, hidden), BF16)],
        scratch_shapes=[pltpu.VMEM(cov.shape, BF16), pltpu.VMEM(sketch.shape, BF16)]
        + scratch
        + [sems, sems],
        compiler_params=params(62),
    )(ids, cov, sketch, weights)
    near = pl.pallas_call(
        functools.partial(near_partial_kernel, half),
        in_specs=[SMEM, VMEM, HBM],
        out_specs=[VMEM] * (half // 2),
        out_shape=[pair] * (half // 2),
        scratch_shapes=scratch + [sems],
        compiler_params=params(),
    )(ids, weighted, weights)
    return [*near, *far]


def cluster_kernel(pairs, ids_ref, member_ref, *refs):
    received, passed, refs = refs[:pairs], refs[pairs : 2 * pairs], refs[2 * pairs :]
    rows_ref, outs, total = refs[0], refs[1 : 1 + pairs], refs[-1]
    me = ids_ref[0]
    total[...] = jnp.zeros_like(total)
    for q in range(pairs):
        for i, ref in enumerate((received[q], passed[q])):
            c = member_ref[me ^ (2 * q + i)]
            total[c] = total[c] + ref[i].astype(F32)
    rows_ref[...] = total[...].astype(BF16)
    for q in range(pairs):
        for i in range(2):
            outs[q][i] = rows_ref[member_ref[me ^ (2 * q + i)]]


def gram_kernel(ids_ref, rows_ref, keep_ref, send_ref):
    half = rows_ref.shape[1] // 2
    kept = keep_ref.shape[0]
    base = base_cluster(ids_ref[0], 4 * kept)
    for k in range(kept):
        for out_ref, slot in ((send_ref, k + kept), (keep_ref, k)):
            block = rows_ref[base ^ slot]
            full = dot(block, block, ((1,), (1,)))
            out_ref[k, 0] = full[:half, :half]
            out_ref[k, 1] = full[half:, :half]
            out_ref[k, 2] = full[half:, half:]


def cluster_sums(ids, members, received, passed):
    pairs = len(received)
    _, rank, rows = received[0].shape
    gram = jax.ShapeDtypeStruct((pairs // 2, 3, rank // 2, rank // 2), F32)
    pair = jax.ShapeDtypeStruct((2, rank, rows), BF16)
    rows_t, *outs = pl.pallas_call(
        functools.partial(cluster_kernel, pairs),
        in_specs=[SMEM, SMEM] + [VMEM] * (2 * pairs),
        out_specs=[VMEM] * (pairs + 1),
        out_shape=[jax.ShapeDtypeStruct((pairs, rank, rows), BF16)] + [pair] * pairs,
        scratch_shapes=[pltpu.VMEM((pairs, rank, rows), F32)],
        compiler_params=params(),
    )(ids, members, *received, *passed)
    keep, send = pl.pallas_call(
        gram_kernel,
        in_specs=[SMEM, VMEM],
        out_specs=[VMEM] * 2,
        out_shape=[gram, gram],
        compiler_params=params(),
    )(ids, rows_t)
    return rows_t, keep, send, outs


def stacked(x, axis, order):
    high = x.astype(BF16)
    rest = x - high.astype(F32)
    middle = rest.astype(BF16)
    low = (rest - middle.astype(F32)).astype(BF16)
    return jnp.concatenate([(high, middle, low)[i] for i in order], axis=axis)


def stack_left(x, axis):
    return stacked(x, axis, (0, 0, 1, 0, 2, 1))


def stack_right(x, axis):
    return stacked(x, axis, (0, 1, 0, 2, 0, 1))


def block_inverse(square):
    size = square.shape[0]
    lanes = 128
    groups = size // 8
    row = lax.broadcasted_iota(jnp.int32, (size, size), 0)
    col = lax.broadcasted_iota(jnp.int32, (size, size), 1)
    parts = [square, jnp.where(row == col, 1.0, 0.0)]
    if lanes > 2 * size:
        parts.append(jnp.zeros((size, lanes - 2 * size), F32))
    table = jnp.concatenate(parts, axis=1)
    tiles = [table[8 * g : 8 * g + 8, :] for g in range(groups)]
    sub = lax.broadcasted_iota(jnp.int32, (8, lanes), 0)
    pivots = [jnp.ones((8, lanes), F32) for _ in range(groups)]

    def spread(x):
        return jnp.broadcast_to(x, (8, lanes))

    for k in range(0, size, PANEL):
        first = k // 8
        columns = [
            [spread(tiles[g][:, k + i : k + i + 1]) for g in range(first, groups)]
            for i in range(PANEL)
        ]
        s = {}
        for m in range(PANEL):
            for i in range(m, PANEL):
                q = k + i
                s[m, i] = spread(columns[m][q // 8 - first][q % 8 : q % 8 + 1, :])
        rows = [spread(tiles[(k + i) // 8][(k + i) % 8 : (k + i) % 8 + 1, :]) for i in range(PANEL)]
        inverse = []
        for m in range(PANEL):
            inverse.append(1.0 / s[m, m])
            for i in range(m + 1, PANEL):
                factor = s[m, i] * inverse[m]
                for t in range(i, PANEL):
                    s[i, t] = s[i, t] - factor * s[m, t]
                rows[i] = rows[i] - factor * rows[m]
        factors = []
        for m in range(PANEL):
            column = []
            for g in range(groups - first):
                x = columns[m][g]
                for t in range(m):
                    x = x - factors[t][g] * s[t, m]
                column.append(x * inverse[m])
            factors.append(column)
        for g in range(first, groups):
            tile = tiles[g]
            for m in range(PANEL):
                x = factors[m][g - first]
                if 8 * g <= k + m:
                    x = jnp.where(sub + 8 * g > k + m, x, 0.0)
                tile = tile - x * rows[m]
            tiles[g] = tile
        for m in range(PANEL):
            q = k + m
            pivots[q // 8] = jnp.where(sub == q % 8, s[m, m], pivots[q // 8])
    out = [tiles[g] * lax.rsqrt(pivots[g]) for g in range(groups)]
    return jnp.concatenate(out, axis=0)[:, size : 2 * size]


def invert(work):
    n = work.shape[0]
    for top in range(0, n, BLOCK):
        left = top // 128 * 128
        bottom = top + BLOCK
        square = work[top:bottom, left : left + 128][:, top - left : bottom - left]
        scaled = dot(
            stack_left(block_inverse(square), 1), stack_right(work[top:bottom, :], 0), ((1,), (0,))
        )
        work[top:bottom, n:] = scaled[:, n:]
        if bottom < n:
            start = bottom // 128 * 128
            change = dot(stack_left(scaled[:, start:n], 0), stack_right(scaled, 0), ((0,), (0,)))
            work[bottom:, :] = work[bottom:, :] - change[bottom - start :, :]


def identity(n):
    row = lax.broadcasted_iota(jnp.int32, (n, n), 0)
    col = lax.broadcasted_iota(jnp.int32, (n, n), 1)
    return jnp.where(row == col, 1.0, 0.0)


def inverse_kernel(scale, gram_ref, rows_t_ref, out_ref, rows_ref, work):
    for c in range(rows_ref.shape[0]):
        rows_ref[c] = rows_t_ref[c].T
    half = gram_ref.shape[1]
    n = 2 * half
    work[:half, :half] = gram_ref[0]
    work[half:, :half] = gram_ref[1]
    work[:half, half:n] = gram_ref[1].T
    work[half:, half:n] = gram_ref[2]
    work[:, n:] = identity(n)
    invert(work)
    out_ref[0] = (scale * work[:half, n : n + half]).astype(BF16)
    out_ref[1] = (scale * work[half:, n : n + half]).astype(BF16)
    out_ref[2] = (scale * work[half:, n + half :]).astype(BF16)


def inverse_factor(gram, rows_t, scale):
    half = gram.shape[1]
    clusters, rank, rows = rows_t.shape
    return pl.pallas_call(
        functools.partial(inverse_kernel, scale),
        in_specs=[VMEM] * 2,
        out_specs=[VMEM] * 2,
        out_shape=[
            jax.ShapeDtypeStruct(gram.shape, BF16),
            jax.ShapeDtypeStruct((clusters, rows, rank), BF16),
        ],
        scratch_shapes=[pltpu.VMEM((2 * half, 4 * half), F32)],
        compiler_params=params(),
        cost_estimate=busy(BUSY["invert"]),
    )(gram, rows_t)


def whole_factor(ref, index):
    first, below, second = (ref[index, i] for i in range(3))
    top = jnp.concatenate([first, jnp.zeros_like(first)], axis=1)
    return jnp.concatenate([top, jnp.concatenate([below, second], axis=1)], axis=0)


def basis_kernel(ids_ref, rows_ref, near_ref, far_ref, out_hbm, out, sems):
    count = near_ref.shape[0]
    base = base_cluster(ids_ref[0], 4 * count)

    def copy(k):
        return pltpu.make_async_copy(out.at[k], out_hbm.at[base ^ k], sems.at[k])

    for k in range(2 * count):
        ref, i = (near_ref, k) if k < count else (far_ref, k - count)
        out[k] = dot(rows_ref[base ^ k], whole_factor(ref, i), ((1,), (1,))).astype(BF16)
        copy(k).start()
    for k in range(2 * count):
        copy(k).wait()


def basis_rows(ids, rows, near, far):
    return pl.pallas_call(
        basis_kernel,
        in_specs=[SMEM] + [VMEM] * 3,
        out_specs=HBM,
        out_shape=jax.ShapeDtypeStruct(rows.shape, BF16),
        scratch_shapes=[pltpu.VMEM(rows.shape, BF16), pltpu.SemaphoreType.DMA((rows.shape[0],))],
        compiler_params=params(),
        cost_estimate=busy(BUSY["basis"]),
    )(ids, rows, near, far)


def column_block(ref, index, rows):
    if rows % 128 == 0:
        return ref[:, pl.ds(pl.multiple_of(index * rows, rows), rows)]
    share = 128 // rows
    wide = ref[:, pl.ds(pl.multiple_of(index // share * 128, 128), 128)]
    block = wide[:, :rows]
    for i in range(1, share):
        block = jnp.where(index % share == i, wide[:, i * rows : (i + 1) * rows], block)
    return block


def slots_of(pairs):
    return [2 * q + i for q in pairs for i in range(2)]


def add_products(total, columns, refs, places):
    for column, (ref, block) in zip(columns, places):
        term = dot(column, refs[ref][block], ((1,), (1,)))
        total = term if total is None else total + term
    return total


def first_product_kernel(early, late, places, ids_ref, weights_hbm, *refs):
    *refs, out_ref, late_ref, weights, sem = refs
    me = ids_ref[0]
    rows = refs[0].shape[2]
    copy = pltpu.make_async_copy(weights_hbm, weights, sem)
    copy.start()
    copy.wait()
    columns = [column_block(weights, me ^ s, rows) for s in slots_of(early)]
    out_ref[...] = add_products(None, columns, refs, places)
    for k, s in enumerate(slots_of(late)):
        late_ref[:, k * rows : (k + 1) * rows] = column_block(weights, me ^ s, rows)


def late_product_kernel(places, weights_ref, first_ref, *refs):
    *refs, high_ref, low_ref = refs
    rows = refs[0].shape[2]
    columns = [weights_ref[:, k * rows : (k + 1) * rows] for k in range(len(places))]
    total = add_products(first_ref[...], columns, refs, places)
    high = total.astype(BF16)
    high_ref[...] = high
    low_ref[...] = (total - high.astype(F32)).astype(BF16)


def coef_kernel(ids_ref, member_ref, high_ref, low_ref, near_ref, far_ref, out_hbm, out, out_sem):
    me = ids_ref[0]
    slot = member_ref[me] ^ base_cluster(me, member_ref.shape[0])
    inside = lax.rem(slot, near_ref.shape[0])
    factor = jnp.where(
        slot < near_ref.shape[0], whole_factor(near_ref, inside), whole_factor(far_ref, inside)
    )
    twice = jnp.concatenate([factor, factor], axis=1)
    part = out.shape[0] // 2
    copies = []
    for i in range(2):
        piece = pl.ds(i * part, part)
        both = jnp.concatenate([high_ref[piece], low_ref[piece]], axis=1)
        out[piece] = dot(both, twice, ((1,), (1,))).astype(BF16)
        copies.append(pltpu.make_async_copy(out.at[piece], out_hbm.at[piece], out_sem.at[i]))
        copies[i].start()
    for copy in copies:
        copy.wait()


def first_product(ids, weights, early, late, arrays, places):
    hidden, width = weights.shape
    _, rank, rows = arrays[0].shape
    return pl.pallas_call(
        functools.partial(first_product_kernel, early, late, places),
        in_specs=[SMEM, HBM] + [VMEM] * len(arrays),
        out_specs=[VMEM] * 2,
        out_shape=[
            jax.ShapeDtypeStruct((hidden, rank), F32),
            jax.ShapeDtypeStruct((hidden, 2 * len(late) * rows), BF16),
        ],
        scratch_shapes=[pltpu.VMEM(weights.shape, BF16), pltpu.SemaphoreType.DMA],
        compiler_params=params(),
        cost_estimate=busy(BUSY["product"]),
    )(ids, weights, *arrays)


def late_product(late_weights, first, arrays, places):
    return pl.pallas_call(
        functools.partial(late_product_kernel, places),
        in_specs=[VMEM] * (len(arrays) + 2),
        out_specs=[VMEM] * 2,
        out_shape=[jax.ShapeDtypeStruct(first.shape, BF16)] * 2,
        compiler_params=params(),
        cost_estimate=busy(BUSY["late"]),
    )(late_weights, first, *arrays)


def coefficients(ids, members, product, near, far):
    out = product[0].shape
    return pl.pallas_call(
        coef_kernel,
        in_specs=[SMEM, SMEM] + [VMEM] * 4,
        out_specs=HBM,
        out_shape=jax.ShapeDtypeStruct(out, BF16),
        scratch_shapes=[pltpu.VMEM(out, BF16), pltpu.SemaphoreType.DMA((2,))],
        compiler_params=params(),
    )(ids, members, *product, near, far)


def swap(block, distance):
    count = lax.axis_size("expert")
    return lax.ppermute(block, "expert", [(i, i ^ distance) for i in range(count)])


def tied(value, values, keys):
    value, *others = lax.optimization_barrier((value, *[values[k] for k in keys]))
    values.update(zip(keys, others))
    return value


def halves(keep, other):
    cut = keep.shape[0] // 2
    first, second = other if isinstance(other, tuple) else (other[:cut], other[cut:])
    return keep[:cut] + first, keep[cut:] + second


def local(down_proj, cov_factor, sketch, membership):
    devices = lax.axis_size("expert")
    weights = down_proj[0]
    width = weights.shape[1]
    last = devices.bit_length() - 2
    half = devices // 2
    me = lax.axis_index("expert")
    ids = me.astype(jnp.int32).reshape(1)

    pairs = devices // 2
    middle = pairs // 2
    blocks = partial_blocks(ids, cov_factor[0], sketch[0], weights, devices)
    got = {0: blocks[0]}
    far = list(range(middle, pairs))
    near = list(range(1, middle))
    share = -(-len(near) // max(1, len(far) - 2))
    for q in far[:2] + near:
        got[q] = swap(blocks[q], 2 * q)
    for k, q in enumerate(far[2:]):
        block = tied(blocks[q], got, [far[k]] + near[k * share : (k + 1) * share])
        got[q] = swap(block, 2 * q)
    every = range(pairs)
    rows_t, keep, send, blocks = cluster_sums(
        ids, membership, [got[q] for q in every], [swap(got[q], 1) for q in every]
    )

    even = [q for q in range(pairs - 1, middle - 1, -1) if q % 2 == 0]
    last_pairs = [q for q in range(middle, pairs) if q % 2]
    inner = list(range(1, middle))
    inner_parts = [q for q in inner if q % 2 == 0], [q for q in inner if q % 4 == 1], [q for q in inner if q % 4 == 3]
    values = {0: blocks[0]}
    passed = {}

    def start(keys, gate):
        for q in keys:
            block, gate = lax.optimization_barrier((blocks[q], gate))
            values[q] = swap(block, 2 * q)
        return gate

    def pass_on(keys):
        pair = values[keys[0]] if len(keys) == 1 else jnp.concatenate([values[q] for q in keys])
        passed[tuple(keys)] = swap(pair, 1)

    def blocks_for(keys):
        groups = [g for g in passed if set(g) <= set(keys)]
        arrays = [values[q] for q in keys] + [passed[g] for g in groups]
        places = []
        for k, q in enumerate(keys):
            (n, g), = ((n, g) for n, g in enumerate(groups) if q in g)
            places += [(k, 0), (len(keys) + n, 2 * g.index(q) + 1)]
        return arrays, places

    share = len(even) // 2
    rows_t = start(inner_parts[0] + even, rows_t)
    other = swap(send, 1)
    for bit in range(1, last):
        keep, send = halves(keep, other)
        if bit == 2:
            for q in even[:share]:
                pass_on([q])
            send = tied(send, values, inner_parts[0])
            send = tied(send, passed, [(q,) for q in even[:share]])
            send = start(inner_parts[1] + inner_parts[2], send)
        if bit == 1 and last > 2:
            cut = send.shape[0] // 2
            other = swap(send[:cut], 1 << bit), swap(send[cut:], 1 << bit)
        else:
            other = swap(send, 1 << bit)
    gram = tied(keep + other, values, even[share:] + inner_parts[1])
    gram = gram + swap(gram, half)
    gram = tied(gram, values, inner_parts[2])

    cut = len(last_pairs) // 2
    early = [q for q in every if q not in last_pairs]
    for q in early:
        if (q,) not in passed:
            values[q], gram = lax.optimization_barrier((values[q], gram))
            pass_on([q])
    gram = start(last_pairs[:cut], gram)
    inverse, rows = inverse_factor(gram[0], rows_t, math.sqrt(width))
    near = tied(inverse[None], passed, list(passed))
    first, late_weights = first_product(ids, weights, early, last_pairs, *blocks_for(early))
    near = start(last_pairs[cut:], near)
    pieces = [near]
    for bit in reversed(range(1, last)):
        if len(pieces) > 2:
            pieces = [jnp.concatenate(pieces, axis=0)]
        pieces += [swap(piece, 1 << bit) for piece in pieces]
        if bit == last - 1:
            pieces[1] = tied(pieces[1], values, last_pairs[:cut])
            pieces[1], first = lax.optimization_barrier((pieces[1], first))
    far = jnp.concatenate([swap(piece, 1) for piece in pieces], axis=0)
    near = jnp.concatenate(pieces, axis=0)
    for q in last_pairs:
        pass_on([q])
    near, far = lax.optimization_barrier((near, far))
    basis = basis_rows(ids, rows, near, far)
    near = tied(near, passed, [(q,) for q in last_pairs[cut:]])
    product = late_product(late_weights, first, *blocks_for(last_pairs))
    coef = coefficients(ids, membership, product, near, far)
    return (coef[None], basis)


def solution(mesh):
    placed = (
        P(("groups", "expert"), None, None),
        P(("groups", "expert"), None, None),
        P(("groups", "expert"), None, None),
        P("groups"),
    )
    return jax.shard_map(
        local,
        mesh=mesh,
        in_specs=placed,
        out_specs=(P(("groups", "expert"), None, None), P("groups", "expert", None)),
        check_vma=False,
    )
```
